256 devices in a mesh: replica: 32 (over z_lo, x, core), fsdp: 8 (over z_hi, y).
Axes of the slice: x: 4, y: 4, z: 8 (z_hi: 2, z_lo: 4; z = z_hi * 4 + z_lo), core: 2. Of those that a mesh axis runs over, the one named last changes fastest.
Arguments:
- pseudo_grad: bfloat16 [32, 1024, 8192], P('replica', 'fsdp'), may hold values from -36 to 36
- anchor: float32 [1024, 8192], P('fsdp', 'replica'), may hold values from -6 to 6
- momentum: float32 [1024, 8192], P('fsdp', 'replica'), may hold values from -4 to 4
- hidden: bfloat16 [32, 3072, 128], P('replica', 'fsdp'), may hold values from -6 to 6
- grad_out: bfloat16 [32, 3072, 8192], P('replica', 'fsdp'), may hold values from -0.109375 to 0.109375
Outputs:
- anchor_next: float32 [1024, 8192], P('fsdp', 'replica')
- momentum_next: float32 [1024, 8192], P('fsdp', 'replica')
- params_next: bfloat16 [1024, 8192], P('fsdp')
- grad_shard: bfloat16 [32, 128, 8192], P('replica', 'fsdp')
The draws below stay inside these ranges and needn't reach their ends.
All inputs are finite; a program needn't handle non-finite values.
Results may differ from the reference program's by a relative error of at most 0.015.
Values may be sent and summed in bfloat16 or wider, within the bound.
No kernel may reach another device: no remote copies, remote signals or barrier semaphores. Data moves between devices by JAX's collectives and lax.ppermute only.
A program may use at most 64 MiB of HBM per device.

```python
import math
import jax
import jax.numpy as jnp
from jax import lax

D = 8192
BLOCK = 128
TOK_DEV = 384
SYNC_ROWS = 1024
WINDOW = 128
TOK_GROUP = 3072
N_REPLICA = 32
N_FSDP = 8


def draw_pseudo_grad(key, part):
    key = jax.random.fold_in(key, 11)
    key_base, key_rows, key_cols = jax.random.split(key, 3)
    shape = (N_REPLICA, SYNC_ROWS, D)
    row_scale = jnp.exp(jax.random.uniform(key_rows, (N_REPLICA, SYNC_ROWS, 1), jnp.float32, math.log(0.3), math.log(3.0)))
    col_scale = jnp.exp(jax.random.uniform(key_cols, (1, 1, D), jnp.float32, math.log(0.3), math.log(3.0)))
    base = jnp.clip(jax.random.normal(key_base, shape, jnp.float32), -4.0, 4.0)
    return (base * row_scale * col_scale).astype(jnp.bfloat16)


def spiked(array, key, source, target, blocks, factor):
    owner, partner = [(jnp.arange(array.shape[position]) // (array.shape[position] // blocks)).reshape([-1 if axis == position else 1 for axis in range(array.ndim)]) for position in (source, target)]
    chosen = jax.random.permutation(key, blocks)[partner]
    strong = (owner == chosen) | (owner == (partner + blocks // 2) % blocks)
    return jnp.where(strong, factor * array, array)


def level_of(own_key, shape, pieces, low, high):
    level, own = 1.0, jax.random.fold_in(own_key, 6)
    for axis_at, parts in pieces:
        draws = jnp.exp(jax.random.uniform(jax.random.fold_in(own, axis_at), (parts,), jnp.float32, low / len(pieces), high / len(pieces)))
        level = level * jnp.repeat(draws, shape[axis_at] // parts).reshape([-1 if axis == axis_at else 1 for axis in range(len(shape))])
    return level


def gaussian(stream_key, extent, spread, bound, shards=(), kind=jnp.bfloat16):
    level = level_of(stream_key, extent, shards, -0.22, 0.18) if shards else 1.0
    values = jax.random.normal(stream_key, extent, jnp.float32) * spread * level
    return jnp.minimum(jnp.maximum(values, -bound), bound).astype(kind)


def bell_draw_with(rng, extent, spread, most, cuts, heavy, kind=jnp.bfloat16):
    entries = spread * jax.random.normal(rng, extent, jnp.float32)
    if cuts:
        entries = entries * level_of(rng, extent, cuts, -0.22, 0.18)
    return jnp.clip(spiked(entries, jax.random.fold_in(rng, 3), *heavy), -most, most).astype(kind)


def setup_inputs(seed: int = 0) -> dict:
    keys = jax.random.split(jax.random.key(seed), 6)
    return {
        "pseudo_grad": draw_pseudo_grad(jax.random.fold_in(keys[5], 71), 0),
        "anchor": gaussian(keys[1], (SYNC_ROWS, D), 1.0, 6.0, ((0, 8), (1, 32)), jnp.float32),
        "momentum": gaussian(keys[2], (SYNC_ROWS, D), 0.3, 4.0, ((0, 8), (1, 32)), jnp.float32),
        "hidden": bell_draw_with(keys[3], (N_REPLICA, TOK_GROUP, WINDOW), 1.0, 6.0, ((0, 32), (1, 8)), (1, 2, 8, 2.0)),
        "grad_out": gaussian(keys[4], (N_REPLICA, TOK_GROUP, D), TOK_GROUP ** -0.5, 0.109375, ((0, 32), (1, 8))),
    }


EPSILON = 1e-6
CODE_TOP = 64.0
OUTER_MOMENTUM = 0.9
OUTER_RATE = 0.7


def power_two(exponent):
    result = jnp.ones(exponent.shape, jnp.float32)
    for bit_pos in range(5):
        chosen = ((exponent >> bit_pos) & 1) == 1
        result = result * jnp.where(chosen, jnp.float32(2.0 ** (2 ** bit_pos)), jnp.float32(1.0))
    return result


def step_scale(peak):
    bounded = peak + EPSILON
    exponent = jnp.floor(jnp.log2(CODE_TOP / bounded)).astype(jnp.int32)
    return power_two(exponent)


def reference(pseudo_grad, anchor, momentum, hidden, grad_out):
    blocks = D // BLOCK
    peak = jnp.max(jnp.abs(pseudo_grad).reshape(N_REPLICA, SYNC_ROWS, blocks, BLOCK), axis=(0, 3)).astype(jnp.float32)
    inv_wide = step_scale(peak)

    def add_code(running, replica_rows):
        product = replica_rows.astype(jnp.float32).reshape(SYNC_ROWS, blocks, BLOCK) * inv_wide[:, :, None]
        encoded = jnp.floor(product + 0.5)
        return running + encoded, None

    running, _ = lax.scan(add_code, jnp.zeros((SYNC_ROWS, blocks, BLOCK), jnp.float32), pseudo_grad)
    delta = (running / (inv_wide[:, :, None] * N_REPLICA)).reshape(SYNC_ROWS, D)
    momentum_next = OUTER_MOMENTUM * momentum + delta
    anchor_next = anchor - OUTER_RATE * (delta + OUTER_MOMENTUM * momentum_next)
    params_next = anchor_next.astype(jnp.bfloat16)

    def one_replica(operands):
        act_rows = operands[0].reshape(N_FSDP, TOK_DEV, WINDOW)
        out_rows = operands[1].reshape(N_FSDP, TOK_DEV, D)

        def add_group(acc, group):
            partial_value = jnp.dot(group[0].T, group[1], preferred_element_type=jnp.float32).astype(jnp.bfloat16)
            partial_value = lax.optimization_barrier(partial_value)
            return acc + partial_value.astype(jnp.float32), None

        acc, _ = lax.scan(add_group, jnp.zeros((WINDOW, D), jnp.float32), (act_rows, out_rows))
        return acc.astype(jnp.bfloat16)

    grad_shard = lax.map(one_replica, (hidden, grad_out))
    return anchor_next, momentum_next, params_next, grad_shard
```

```python
import functools

import jax
import jax.numpy as jnp
from jax import lax
from jax.experimental import pallas as pl
from jax.experimental.pallas import tpu as pltpu
from jax.sharding import PartitionSpec as P

BLOCK = 128
EPSILON = 1e-06
TOP_EXPONENT = 6
OUTER_MOMENTUM = 0.9
OUTER_RATE = 0.7
LIMIT = 16 * 1024 * 1024

ANY = pl.BlockSpec(memory_space=pl.ANY)
VMEM = pl.BlockSpec(memory_space=pltpu.VMEM)
SMEM = pl.BlockSpec(memory_space=pltpu.SMEM)


def replica_perm(move):
    pairs = []
    for z in range(4):
        for x in range(4):
            for c in range(2):
                to = move(z, x, c)
                pairs.append((z * 8 + x * 2 + c, to[0] * 8 + to[1] * 2 + to[2]))
    return pairs


def fsdp_perm(move):
    pairs = []
    for h in range(2):
        for y in range(4):
            to = move(h, y)
            pairs.append((h * 4 + y, to[0] * 4 + to[1]))
    return pairs


def to_core(a):
    return lax.ppermute(a, "replica", replica_perm(lambda z, x, c: (z, x, 1 - c)))


def to_x(a, k):
    return lax.ppermute(a, "replica", replica_perm(lambda z, x, c: (z, (x + k) % 4, c)))


def to_z(a, k):
    return lax.ppermute(a, "replica", replica_perm(lambda z, x, c: (z ^ k, x, c)))


def to_y(a, k):
    return lax.ppermute(a, "fsdp", fsdp_perm(lambda h, y: (h, (y + k) % 4)))


def to_half(a):
    return lax.ppermute(a, "fsdp", fsdp_perm(lambda h, y: (1 - h, y)))


def call(kernel, out, ins, specs, out_specs=None, scratch=(), cost=0, alias=None):
    return pl.pallas_call(
        kernel,
        out_shape=out,
        in_specs=specs,
        out_specs=out_specs if out_specs is not None else [VMEM] * len(out),
        scratch_shapes=list(scratch),
        input_output_aliases=alias or {},
        cost_estimate=pl.CostEstimate(flops=cost, bytes_accessed=cost, transcendentals=0),
        compiler_params=pltpu.CompilerParams(vmem_limit_bytes=LIMIT),
    )(*ins)


def bf16(*shape):
    return jax.ShapeDtypeStruct(shape, jnp.bfloat16)


def f32(*shape):
    return jax.ShapeDtypeStruct(shape, jnp.float32)


def split_kernel(where, grad, keep, give, sems):
    core = where[0]
    copies = []
    for n in range(16):
        for side, out in ((1 - core, give), (core, keep)):
            start = pl.multiple_of(n * 512 + side * 256, 256)
            copies.append((grad.at[0, :, pl.ds(start, 256)], out.at[n]))
    flat = [
        pltpu.make_async_copy(src, dst, sems.at[i]) for i, (src, dst) in enumerate(copies)
    ]
    for copy in flat:
        copy.start()
    for copy in flat:
        copy.wait()


def peak_kernel(mine, other, out):
    lanes = lax.broadcasted_iota(jnp.int32, (128, 128), 1)
    acc = jnp.zeros((128, 128), jnp.float32)
    for n in range(16):
        for b in range(2):
            cols = slice(b * BLOCK, (b + 1) * BLOCK)
            both = jnp.maximum(jnp.abs(mine[n, :, cols]), jnp.abs(other[n, :, cols]))
            top = jnp.max(both.astype(jnp.float32), axis=1, keepdims=True)
            acc = jnp.where(lanes == 2 * n + b, top, acc)
    out[...] = acc.T[:32].astype(jnp.bfloat16)


def scale_of(peak):
    bounded = peak + EPSILON
    scale = jnp.ones_like(bounded)
    for e in range(1, 26):
        scale = jnp.where(bounded <= 2.0 ** (TOP_EXPONENT - e), 2.0**e, scale)
    return scale


def encode_kernel(where, mine, other, p0, p1, p2, p3, o0, o1, o2, o3, step, scales):
    x, z = where[1], where[2]
    peak = jnp.maximum(
        jnp.maximum(p0[...].astype(jnp.float32), p1[...].astype(jnp.float32)),
        jnp.maximum(p2[...].astype(jnp.float32), p3[...].astype(jnp.float32)),
    )
    scale = scale_of(peak)
    wide = jnp.concatenate([scale, jnp.ones((96, 128), jnp.float32)], axis=0).T
    for n in range(32):
        scales[n // 2, :, (n % 2) * BLOCK : (n % 2 + 1) * BLOCK] = jnp.broadcast_to(
            wide[:, n : n + 1], (128, 128)
        )
    step[...] = 1.0 / (scales[z * 4 + x] * 32.0)
    for k, out in enumerate((o0, o1, o2, o3)):
        column = lax.rem(x + k, 4)
        for level in range(4):
            n = level * 4 + column
            s = scales[n]
            first = jnp.floor(mine[n].astype(jnp.float32) * s + 0.5)
            second = jnp.floor(other[n].astype(jnp.float32) * s + 0.5)
            out[level] = (first + second).astype(jnp.bfloat16)


def sum_x_kernel(where, a0, a1, a2, a3, o0, o1, o2, o3):
    z = where[2]
    for k, out in enumerate((o0, o1, o2, o3)):
        level = z ^ k
        parts = [a[level].astype(jnp.float32) for a in (a0, a1, a2, a3)]
        out[...] = (((parts[0] + parts[1]) + (parts[2] + parts[3]))).astype(out.dtype)


def update_kernel(a0, a1, a2, a3, step, anchor, momentum, anchor_out, momentum_out, params):
    parts = [a[...].astype(jnp.float32) for a in (a0, a1, a2, a3)]
    total = (parts[0] + parts[1]) + (parts[2] + parts[3])
    delta = total * step[...]
    fresh = OUTER_MOMENTUM * momentum[...] + delta
    moved = anchor[...] - OUTER_RATE * (delta + OUTER_MOMENTUM * fresh)
    momentum_out[...] = fresh
    anchor_out[...] = moved
    params[...] = moved.astype(jnp.bfloat16)


def gather_z_kernel(where, a0, a1, a2, a3, out):
    z = where[2]
    for k, a in enumerate((a0, a1, a2, a3)):
        out[z ^ k] = a[...]


def gather_x_kernel(where, a0, a1, a2, a3, out):
    x = where[1]
    for k, a in enumerate((a0, a1, a2, a3)):
        column = lax.rem(x + 4 - k, 4)
        for level in range(4):
            out[level * 4 + column] = a[level]


def place_kernel(where, mine, other, out, sems):
    core = where[0]
    copies = []
    for n in range(16):
        for side, src in ((core, mine), (1 - core, other)):
            start = pl.multiple_of(n * 512 + side * 256, 256)
            copies.append((src.at[n], out.at[:, pl.ds(start, 256)]))
    flat = [
        pltpu.make_async_copy(src, dst, sems.at[i]) for i, (src, dst) in enumerate(copies)
    ]
    for copy in flat:
        copy.start()
    for copy in flat:
        copy.wait()


def outer_sync(where, pseudo_grad, anchor, momentum):
    mine, give = call(
        split_kernel,
        [bf16(16, 128, 256)] * 2,
        (where, pseudo_grad),
        [SMEM, ANY],
        scratch=[pltpu.SemaphoreType.DMA((32,))],
        cost=1 << 21,
    )
    other = to_core(give)
    (peak,) = call(peak_kernel, [bf16(32, 128)], (mine, other), [VMEM] * 2, cost=1 << 21)
    for k in range(0, 1):
        near = [to_x(peak, k) for k in (1, 2, 3)]
        peak = jnp.maximum(jnp.maximum(peak, near[0]), jnp.maximum(near[1], near[2]))
    peaks = [peak] + [to_z(peak, k) for k in (1, 2, 3)]
    *codes, step = call(
        encode_kernel,
        [bf16(4, 128, 256)] * 4 + [f32(128, 256)],
        (where, mine, other, *peaks),
        [SMEM] + [VMEM] * 6,
        scratch=[pltpu.VMEM((16, 128, 256), jnp.float32)],
        cost=1 << 22,
    )
    parts = [codes[0]] + [to_x(codes[k], k) for k in (1, 2, 3)]
    sums = call(
        sum_x_kernel,
        [f32(128, 256)] + [bf16(128, 256)] * 3,
        (where, *parts),
        [SMEM] + [VMEM] * 4,
        cost=1 << 20,
    )
    parts = [sums[0]] + [to_z(sums[k], k) for k in (1, 2, 3)]
    anchor_next, momentum_next, params = call(
        update_kernel,
        [f32(128, 256), f32(128, 256), bf16(128, 256)],
        (*parts, step, anchor, momentum),
        [VMEM] * 7,
        cost=1 << 19,
    )
    parts = [params] + [to_z(params, k) for k in (1, 2, 3)]
    (params,) = call(gather_z_kernel, [bf16(4, 128, 256)], (where, *parts), [SMEM] + [VMEM] * 4)
    parts = [params] + [to_x(params, k) for k in (1, 2, 3)]
    (params,) = call(gather_x_kernel, [bf16(16, 128, 256)], (where, *parts), [SMEM] + [VMEM] * 4)
    (params_next,) = call(
        place_kernel,
        [bf16(128, 8192)],
        (where, params, to_core(params)),
        [SMEM, VMEM, VMEM],
        [ANY],
        scratch=[pltpu.SemaphoreType.DMA((32,))],
        cost=1 << 21,
    )
    return anchor_next, momentum_next, params_next


def inner_grad(hidden, grad_out):
    y = lax.rem(lax.axis_index("fsdp"), 4)
    half = lax.div(lax.axis_index("fsdp"), 4)
    partial = lax.dot_general(
        hidden[0], grad_out[0], (((0,), (0,)), ((), ())), preferred_element_type=jnp.float32
    ).astype(jnp.bfloat16)
    partial = partial.reshape(2, 4, 16, -1)
    pieces = [
        lax.dynamic_index_in_dim(partial, lax.rem(y + k, 4), 1, keepdims=False) for k in range(4)
    ]
    pieces = [pieces[0]] + [to_y(pieces[k], k) for k in (1, 2, 3)]
    total = sum(piece.astype(jnp.float32) for piece in pieces)
    keep = lax.dynamic_index_in_dim(total, half, 0, keepdims=False)
    give = lax.dynamic_index_in_dim(total, 1 - half, 0, keepdims=False).astype(jnp.bfloat16)
    return (keep + to_half(give).astype(jnp.float32)).astype(jnp.bfloat16)[None]


def on_device(pseudo_grad, anchor, momentum, hidden, grad_out):
    r = lax.axis_index("replica")
    where = jnp.stack([lax.rem(r, 2), lax.rem(lax.div(r, 2), 4), lax.div(r, 8)]).astype(jnp.int32)
    grad_shard = inner_grad(hidden, grad_out)
    return *outer_sync(where, pseudo_grad, anchor, momentum), grad_shard


def solution(mesh):
    placed = (
        P("replica", "fsdp", None),
        P("fsdp", "replica"),
        P("fsdp", "replica"),
        P("replica", "fsdp", None),
        P("replica", "fsdp", None),
    )
    return jax.shard_map(
        on_device,
        mesh=mesh,
        in_specs=placed,
        out_specs=(
            P("fsdp", "replica"),
            P("fsdp", "replica"),
            P("fsdp", None),
            P("replica", "fsdp", None),
        ),
        check_vma=False,
    )
```

```python
import functools

import jax
import jax.numpy as jnp
from jax import lax
from jax.experimental import pallas as pl
from jax.experimental.pallas import tpu as pltpu
from jax.sharding import PartitionSpec as P

BLOCK = 128
EPSILON = 1e-06
TOP_EXPONENT = 6
OUTER_MOMENTUM = 0.9
OUTER_RATE = 0.7
LIMIT = 16 * 1024 * 1024

ANY = pl.BlockSpec(memory_space=pl.ANY)
VMEM = pl.BlockSpec(memory_space=pltpu.VMEM)
HBM = pl.BlockSpec(memory_space=pltpu.HBM)
SMEM = pl.BlockSpec(memory_space=pltpu.SMEM)


def replica_perm(move):
    pairs = []
    for z in range(4):
        for x in range(4):
            for c in range(2):
                to = move(z, x, c)
                pairs.append((z * 8 + x * 2 + c, to[0] * 8 + to[1] * 2 + to[2]))
    return pairs


def fsdp_perm(move):
    pairs = []
    for h in range(2):
        for y in range(4):
            to = move(h, y)
            pairs.append((h * 4 + y, to[0] * 4 + to[1]))
    return pairs


def to_core(a):
    return lax.ppermute(a, "replica", replica_perm(lambda z, x, c: (z, x, 1 - c)))


def to_x(a, k):
    return lax.ppermute(a, "replica", replica_perm(lambda z, x, c: (z, (x + k) % 4, c)))


def to_z(a, k):
    return lax.ppermute(a, "replica", replica_perm(lambda z, x, c: (z ^ k, x, c)))


def to_y(a, k):
    return lax.ppermute(a, "fsdp", fsdp_perm(lambda h, y: (h, (y + k) % 4)))


def to_half(a):
    return lax.ppermute(a, "fsdp", fsdp_perm(lambda h, y: (1 - h, y)))


def call(kernel, out, ins, specs, out_specs=None, scratch=(), cost=0, alias=None):
    return pl.pallas_call(
        kernel,
        out_shape=out,
        in_specs=specs,
        out_specs=out_specs if out_specs is not None else [VMEM] * len(out),
        scratch_shapes=list(scratch),
        input_output_aliases=alias or {},
        cost_estimate=pl.CostEstimate(flops=cost, bytes_accessed=cost, transcendentals=0),
        compiler_params=pltpu.CompilerParams(vmem_limit_bytes=LIMIT),
    )(*ins)


def gate_kernel(*refs):
    pass


def gate(after, *arrays):
    n = len(arrays)
    return call(
        gate_kernel,
        [jax.ShapeDtypeStruct(a.shape, a.dtype) for a in arrays],
        (*arrays, after),
        [ANY] * (n + 1),
        [ANY] * n,
        cost=1 << 10,
        alias={i: i for i in range(n)},
    )


def bf16(*shape):
    return jax.ShapeDtypeStruct(shape, jnp.bfloat16)


def f32(*shape):
    return jax.ShapeDtypeStruct(shape, jnp.float32)


def split_kernel(where, grad, keep, give, keep_peak, give_peak, sems):
    core = where[0]
    copies = []
    for n in range(16):
        pair = []
        for i, (side, out) in enumerate(((core, keep), (1 - core, give))):
            start = pl.multiple_of(n * 512 + side * 256, 256)
            copy = pltpu.make_async_copy(
                grad.at[0, :, pl.ds(start, 256)], out.at[n], sems.at[2 * n + i]
            )
            copy.start()
            pair.append(copy)
        copies.append(pair)
    lanes = lax.broadcasted_iota(jnp.int32, (128, 128), 1)
    acc = jnp.zeros((128, 128), jnp.float32)
    for n in range(16):
        for i, out in enumerate((keep, give)):
            copies[n][i].wait()
            for b in range(2):
                size = jnp.abs(out[n, :, b * BLOCK : (b + 1) * BLOCK])
                top = jnp.max(size.astype(jnp.float32), axis=1, keepdims=True)
                acc = jnp.where(lanes == 32 * i + 2 * n + b, top, acc)
    flat = acc.T
    keep_peak[...] = flat[:32].astype(jnp.bfloat16)
    give_peak[...] = flat[32:64].astype(jnp.bfloat16)


def top_kernel(a0, a1, a2, a3, *rest):
    out = rest[-1]
    out[...] = jnp.maximum(jnp.maximum(a0[...], a1[...]), jnp.maximum(a2[...], a3[...]))


def scale_of(peak):
    bounded = peak + EPSILON
    scale = jnp.ones_like(bounded)
    for e in range(1, 26):
        scale = jnp.where(bounded <= 2.0 ** (TOP_EXPONENT - e), 2.0**e, scale)
    return scale


def encode_kernel(where, mine, other, p0, p1, p2, p3, o0, o1, o2, o3, step, scales):
    x, z = where[1], where[2]
    peak = jnp.maximum(
        jnp.maximum(p0[...].astype(jnp.float32), p1[...].astype(jnp.float32)),
        jnp.maximum(p2[...].astype(jnp.float32), p3[...].astype(jnp.float32)),
    )
    scale = scale_of(peak)
    wide = jnp.concatenate([scale, jnp.ones((96, 128), jnp.float32)], axis=0).T
    for n in range(32):
        scales[n // 2, :, (n % 2) * BLOCK : (n % 2 + 1) * BLOCK] = jnp.broadcast_to(
            wide[:, n : n + 1], (128, 128)
        )
    step[...] = 1.0 / (scales[z * 4 + x] * 32.0)
    for k, out in enumerate((o0, o1, o2, o3)):
        column = lax.rem(x + k, 4)
        for level in range(4):
            n = level * 4 + column
            s = scales[n]
            first = jnp.floor(mine[n].astype(jnp.float32) * s + 0.5)
            second = jnp.floor(other[n].astype(jnp.float32) * s + 0.5)
            out[level] = (first + second).astype(jnp.bfloat16)


def sum_x_kernel(where, a0, a1, a2, a3, after1, after2, o0, o1, o2, o3):
    z = where[2]
    for k, out in enumerate((o0, o1, o2, o3)):
        level = z ^ k
        parts = [a[level].astype(jnp.float32) for a in (a0, a1, a2, a3)]
        out[...] = (((parts[0] + parts[1]) + (parts[2] + parts[3]))).astype(out.dtype)


def update_kernel(a0, a1, a2, a3, step, anchor, momentum, anchor_out, momentum_out, params):
    parts = [a[...].astype(jnp.float32) for a in (a0, a1, a2, a3)]
    total = (parts[0] + parts[1]) + (parts[2] + parts[3])
    delta = total * step[...]
    fresh = OUTER_MOMENTUM * momentum[...] + delta
    moved = anchor[...] - OUTER_RATE * (delta + OUTER_MOMENTUM * fresh)
    momentum_out[...] = fresh
    anchor_out[...] = moved
    params[...] = moved.astype(jnp.bfloat16)


def gather_z_kernel(where, a0, a1, a2, a3, after, out):
    z = where[2]
    for k, a in enumerate((a0, a1, a2, a3)):
        out[z ^ k] = a[...]


def place_kernel(sides, turns, where, *refs):
    blocks, out, sems = refs[: len(sides)], refs[-2], refs[-1]
    core, x = where[0], where[1]
    copies = []
    for block, side, turn in zip(blocks, sides, turns):
        column = lax.rem(x + 4 - turn, 4)
        half = core if side == 0 else 1 - core
        for level in range(4):
            start = pl.multiple_of((level * 4 + column) * 512 + half * 256, 256)
            copies.append(
                pltpu.make_async_copy(
                    block.at[level], out.at[:, pl.ds(start, 256)], sems.at[len(copies)]
                )
            )
    for copy in copies:
        copy.start()
    for copy in copies:
        copy.wait()


def place(where, out, items):
    blocks, sides, turns = zip(*items)
    given = [] if out is None else [out]
    return call(
        functools.partial(place_kernel, sides, turns),
        [bf16(128, 8192)],
        (where, *blocks, *given),
        [SMEM] + [VMEM] * len(blocks) + [HBM] * len(given),
        [HBM],
        scratch=[pltpu.SemaphoreType.DMA((4 * len(blocks),))],
        cost=1 << 18,
        alias={1 + len(blocks): 0} if given else None,
    )[0]


def both_steps(where, pseudo_grad, anchor, momentum, hidden, grad_out):
    mine, give, peak, other_peak = call(
        split_kernel,
        [bf16(16, 128, 256)] * 2 + [bf16(32, 128)] * 2,
        (where, pltpu.with_memory_space_constraint(pseudo_grad, pltpu.HBM)),
        [SMEM, HBM],
        scratch=[pltpu.SemaphoreType.DMA((32,))],
        cost=1 << 21,
    )
    peak = jnp.maximum(peak, to_core(other_peak))
    other = to_core(give)
    near = [to_x(peak, k) for k in (1, 2, 3)]
    pieces = list(inner_pieces(where, hidden, grad_out, peak))
    (peak,) = call(
        top_kernel,
        [bf16(32, 128)],
        (peak, *near, other, pieces[0]),
        [VMEM] * 4 + [ANY] * 2,
        cost=1 << 16,
    )
    peaks = [peak] + [to_z(peak, k) for k in (1, 2, 3)]
    pieces[1], pieces[2] = gate(peak, pieces[1], pieces[2])
    *codes, step = call(
        encode_kernel,
        [bf16(4, 128, 256)] * 4 + [f32(128, 256)],
        (where, mine, other, *peaks),
        [SMEM] + [VMEM] * 6,
        scratch=[pltpu.VMEM((16, 128, 256), jnp.float32)],
        cost=1 << 22,
    )
    parts = [codes[0]] + [to_x(codes[k], k) for k in (1, 2, 3)]
    pieces[1], pieces[2] = to_y(pieces[1], 1), to_y(pieces[2], 2)
    sums = call(
        sum_x_kernel,
        [f32(128, 256)] + [bf16(128, 256)] * 3,
        (where, *parts, pieces[1], pieces[2]),
        [SMEM] + [VMEM] * 4 + [ANY] * 2,
        cost=1 << 20,
    )
    (pieces[3],) = gate(sums[0], pieces[3])
    inner_keep, inner_give = call(
        sum_y_kernel,
        [f32(16, 8192), bf16(16, 8192)],
        (where, *pieces[:3], to_y(pieces[3], 3)),
        [SMEM] + [VMEM] * 4,
        cost=1 << 21,
    )
    parts = [sums[0]] + [to_z(sums[k], k) for k in (1, 2, 3)]
    anchor_next, momentum_next, params = call(
        update_kernel,
        [f32(128, 256), f32(128, 256), bf16(128, 256)],
        (*parts, step, anchor, momentum),
        [VMEM] * 7,
        cost=1 << 19,
    )
    parts = [params] + [to_z(params, k) for k in (1, 2, 3)]
    (block,) = call(
        gather_z_kernel,
        [bf16(4, 128, 256)],
        (where, *parts, inner_give),
        [SMEM] + [VMEM] * 4 + [ANY],
    )
    far = [to_x(block, k) for k in (1, 2, 3)]
    twin = to_core(block)
    params_next = place(where, None, [(block, 0, 0), (twin, 1, 0)])
    twins = [to_core(a) for a in far]
    params_next = place(where, params_next, [(a, 0, k) for k, a in zip((1, 2, 3), far)])
    params_next = place(where, params_next, [(a, 1, k) for k, a in zip((1, 2, 3), twins)])
    grad_shard = (inner_keep + to_half(inner_give).astype(jnp.float32)).astype(jnp.bfloat16)
    return anchor_next, momentum_next, params_next, grad_shard[None]


def product_kernel(where, hidden, grad, after, o0, o1, o2, o3, left, whole):
    @pl.when(pl.program_id(0) == 0)
    def _():
        left[...] = hidden[0].astype(jnp.float32).T.astype(jnp.bfloat16)

    whole[...] = jnp.dot(
        left[...], grad[0], preferred_element_type=jnp.float32
    ).astype(jnp.bfloat16)
    y = where[3]
    for k, out in enumerate((o0, o1, o2, o3)):
        for half in range(2):
            start = pl.multiple_of(half * 64 + lax.rem(y + k, 4) * 16, 16)
            out[half * 16 : half * 16 + 16, :] = whole[pl.ds(start, 16), :]


def sum_y_kernel(where, a0, a1, a2, a3, keep, give):
    half = where[4]
    for side, out in ((half, keep), (1 - half, give)):
        rows = pl.ds(pl.multiple_of(side * 16, 16), 16)
        parts = [a[rows, :].astype(jnp.float32) for a in (a0, a1, a2, a3)]
        out[...] = ((parts[0] + parts[1]) + (parts[2] + parts[3])).astype(out.dtype)


def inner_pieces(where, hidden, grad_out, after):
    tile = 1024
    return pl.pallas_call(
        product_kernel,
        grid=(8192 // tile,),
        out_shape=[bf16(32, 8192)] * 4,
        in_specs=[
            SMEM,
            pl.BlockSpec((1, 384, 128), lambda i: (0, 0, 0)),
            pl.BlockSpec((1, 384, tile), lambda i: (0, 0, i)),
            ANY,
        ],
        out_specs=[pl.BlockSpec((32, tile), lambda i: (0, i))] * 4,
        scratch_shapes=[
            pltpu.VMEM((128, 384), jnp.bfloat16),
            pltpu.VMEM((128, tile), jnp.bfloat16),
        ],
        cost_estimate=pl.CostEstimate(
            flops=2 * 128 * 384 * 8192, bytes_accessed=1 << 23, transcendentals=0
        ),
        compiler_params=pltpu.CompilerParams(vmem_limit_bytes=LIMIT),
    )(where, hidden, pltpu.with_memory_space_constraint(grad_out, pltpu.HBM), after)


def on_device(pseudo_grad, anchor, momentum, hidden, grad_out):
    r, f = lax.axis_index("replica"), lax.axis_index("fsdp")
    where = jnp.stack([r & 1, (r >> 1) & 3, r >> 3, f & 3, f >> 2]).astype(jnp.int32)
    return both_steps(where, pseudo_grad, anchor, momentum, hidden, grad_out)


def solution(mesh):
    placed = (
        P("replica", "fsdp", None),
        P("fsdp", "replica"),
        P("fsdp", "replica"),
        P("replica", "fsdp", None),
        P("replica", "fsdp", None),
    )
    return jax.shard_map(
        on_device,
        mesh=mesh,
        in_specs=placed,
        out_specs=(
            P("fsdp", "replica"),
            P("fsdp", "replica"),
            P("fsdp", None),
            P("replica", "fsdp", None),
        ),
        check_vma=False,
    )
```

```python
import functools

import jax
import jax.numpy as jnp
from jax import lax
from jax.experimental import pallas as pl
from jax.experimental.pallas import tpu as pltpu
from jax.sharding import PartitionSpec as P

BLOCK = 128
EPSILON = 1e-06
TOP_EXPONENT = 6
OUTER_MOMENTUM = 0.9
OUTER_RATE = 0.7
LIMIT = 16 * 1024 * 1024

ANY = pl.BlockSpec(memory_space=pl.ANY)
VMEM = pl.BlockSpec(memory_space=pltpu.VMEM)
HBM = pl.BlockSpec(memory_space=pltpu.HBM)
SMEM = pl.BlockSpec(memory_space=pltpu.SMEM)


def replica_perm(move):
    pairs = []
    for z in range(4):
        for x in range(4):
            for c in range(2):
                to = move(z, x, c)
                pairs.append((z * 8 + x * 2 + c, to[0] * 8 + to[1] * 2 + to[2]))
    return pairs


def fsdp_perm(move):
    pairs = []
    for h in range(2):
        for y in range(4):
            to = move(h, y)
            pairs.append((h * 4 + y, to[0] * 4 + to[1]))
    return pairs


def to_core(a):
    return lax.ppermute(a, "replica", replica_perm(lambda z, x, c: (z, x, 1 - c)))


def to_x(a, k):
    return lax.ppermute(a, "replica", replica_perm(lambda z, x, c: (z, (x + k) % 4, c)))


def to_z(a, k):
    return lax.ppermute(a, "replica", replica_perm(lambda z, x, c: (z ^ k, x, c)))


def to_y(a, k):
    return lax.ppermute(a, "fsdp", fsdp_perm(lambda h, y: (h, (y + k) % 4)))


def to_half(a):
    return lax.ppermute(a, "fsdp", fsdp_perm(lambda h, y: (1 - h, y)))


def call(kernel, out, ins, specs, out_specs=None, scratch=(), cost=0, alias=None):
    return pl.pallas_call(
        kernel,
        out_shape=out,
        in_specs=specs,
        out_specs=out_specs if out_specs is not None else [VMEM] * len(out),
        scratch_shapes=list(scratch),
        input_output_aliases=alias or {},
        cost_estimate=pl.CostEstimate(flops=cost, bytes_accessed=cost, transcendentals=0),
        compiler_params=pltpu.CompilerParams(vmem_limit_bytes=LIMIT),
    )(*ins)


def gate_kernel(*refs):
    pass


def gate(after, *arrays):
    n = len(arrays)
    return call(
        gate_kernel,
        [jax.ShapeDtypeStruct(a.shape, a.dtype) for a in arrays],
        (*arrays, after),
        [ANY] * (n + 1),
        [ANY] * n,
        cost=1 << 10,
        alias={i: i for i in range(n)},
    )


def bf16(*shape):
    return jax.ShapeDtypeStruct(shape, jnp.bfloat16)


def f32(*shape):
    return jax.ShapeDtypeStruct(shape, jnp.float32)


def split_kernel(where, grad, keep, give, keep_peak, give_peak, rows, tops, sems):
    core = where[0]

    def fetch(i):
        part = pl.ds(pl.multiple_of(i * 16, 16), 16)
        return pltpu.make_async_copy(grad.at[0, part, :], rows.at[part, :], sems.at[i])

    for i in range(8):
        fetch(i).start()
    lanes = lax.broadcasted_iota(jnp.int32, (16, 128), 1)

    def chunk(i, carry):
        fetch(i).wait()
        part = pl.ds(pl.multiple_of(i * 16, 16), 16)
        acc = jnp.zeros((16, 128), jnp.float32)
        for n in range(16):
            for k, (side, out) in enumerate(((core, keep), (1 - core, give))):
                start = pl.multiple_of(n * 512 + side * 256, 256)
                value = rows[part, pl.ds(start, 256)]
                out[n, part, :] = value
                size = jnp.abs(value)
                for b in range(2):
                    block = size[:, b * BLOCK : (b + 1) * BLOCK].astype(jnp.float32)
                    top = jnp.max(block, axis=1, keepdims=True)
                    acc = jnp.where(lanes == 32 * k + 2 * n + b, top, acc)
        tops[part, :] = acc
        return carry

    lax.fori_loop(0, 8, chunk, 0)
    flat = tops[...].T
    keep_peak[...] = flat[:32].astype(jnp.bfloat16)
    give_peak[...] = flat[32:64].astype(jnp.bfloat16)


def top_kernel(a0, a1, a2, a3, *rest):
    out = rest[-1]
    out[...] = jnp.maximum(jnp.maximum(a0[...], a1[...]), jnp.maximum(a2[...], a3[...]))


def scale_of(peak):
    bounded = peak + EPSILON
    scale = jnp.ones_like(bounded)
    for e in range(1, 26):
        scale = jnp.where(bounded <= 2.0 ** (TOP_EXPONENT - e), 2.0**e, scale)
    return scale


def encode_kernel(where, mine, other, p0, p1, p2, p3, after, o0, o1, o2, o3, step, scales):
    x, z = where[1], where[2]
    peak = jnp.maximum(
        jnp.maximum(p0[...].astype(jnp.float32), p1[...].astype(jnp.float32)),
        jnp.maximum(p2[...].astype(jnp.float32), p3[...].astype(jnp.float32)),
    )
    scale = scale_of(peak)
    wide = jnp.concatenate([scale, jnp.ones((96, 128), jnp.float32)], axis=0).T
    for n in range(32):
        scales[n // 2, :, (n % 2) * BLOCK : (n % 2 + 1) * BLOCK] = jnp.broadcast_to(
            wide[:, n : n + 1], (128, 128)
        )
    step[...] = 1.0 / (scales[z * 4 + x] * 32.0)
    for k, out in enumerate((o0, o1, o2, o3)):
        column = lax.rem(x + k, 4)
        for level in range(4):
            n = level * 4 + column
            s = scales[n]
            first = jnp.floor(mine[n].astype(jnp.float32) * s + 0.5)
            second = jnp.floor(other[n].astype(jnp.float32) * s + 0.5)
            out[level] = (first + second).astype(jnp.bfloat16)


def sum_x_kernel(where, a0, a1, a2, a3, o0, o1, o2, o3):
    z = where[2]
    for k, out in enumerate((o0, o1, o2, o3)):
        level = z ^ k
        parts = [a[level].astype(jnp.float32) for a in (a0, a1, a2, a3)]
        out[...] = (((parts[0] + parts[1]) + (parts[2] + parts[3]))).astype(out.dtype)


def update_kernel(a0, a1, a2, a3, step, anchor, momentum, after1, after2, anchor_out, momentum_out, params):
    parts = [a[...].astype(jnp.float32) for a in (a0, a1, a2, a3)]
    total = (parts[0] + parts[1]) + (parts[2] + parts[3])
    delta = total * step[...]
    fresh = OUTER_MOMENTUM * momentum[...] + delta
    moved = anchor[...] - OUTER_RATE * (delta + OUTER_MOMENTUM * fresh)
    momentum_out[...] = fresh
    anchor_out[...] = moved
    params[...] = moved.astype(jnp.bfloat16)


def gather_z_kernel(where, a0, a1, a2, a3, after, out):
    z = where[2]
    for k, a in enumerate((a0, a1, a2, a3)):
        out[z ^ k] = a[...]


def place_kernel(sides, turns, where, *refs):
    blocks, out, sems = refs[: len(sides)], refs[-2], refs[-1]
    core, x = where[0], where[1]
    copies = []
    for block, side, turn in zip(blocks, sides, turns):
        column = lax.rem(x + 4 - turn, 4)
        half = core if side == 0 else 1 - core
        for level in range(4):
            start = pl.multiple_of((level * 4 + column) * 512 + half * 256, 256)
            copies.append(
                pltpu.make_async_copy(
                    block.at[level], out.at[:, pl.ds(start, 256)], sems.at[len(copies)]
                )
            )
    for copy in copies:
        copy.start()
    for copy in copies:
        copy.wait()


def place(where, out, items):
    blocks, sides, turns = zip(*items)
    given = [] if out is None else [out]
    return call(
        functools.partial(place_kernel, sides, turns),
        [bf16(128, 8192)],
        (where, *blocks, *given),
        [SMEM] + [VMEM] * len(blocks) + [HBM] * len(given),
        [HBM],
        scratch=[pltpu.SemaphoreType.DMA((4 * len(blocks),))],
        cost=1 << 18,
        alias={1 + len(blocks): 0} if given else None,
    )[0]


def both_steps(where, pseudo_grad, anchor, momentum, hidden, grad_out):
    mine, give, peak, other_peak = call(
        split_kernel,
        [bf16(16, 128, 256)] * 2 + [bf16(32, 128)] * 2,
        (where, pltpu.with_memory_space_constraint(pseudo_grad, pltpu.HBM)),
        [SMEM, HBM],
        scratch=[
            pltpu.VMEM((128, 8192), jnp.bfloat16),
            pltpu.VMEM((128, 128), jnp.float32),
            pltpu.SemaphoreType.DMA((8,)),
        ],
        cost=1 << 21,
    )
    peak = jnp.maximum(peak, to_core(other_peak))
    other = to_core(give)
    near = [to_x(peak, k) for k in (1, 2, 3)]
    pieces = inner_pieces(where, hidden, grad_out, peak, 0)
    (peak,) = call(
        top_kernel,
        [bf16(32, 128)],
        (peak, *near, other, pieces[0]),
        [VMEM] * 4 + [ANY] * 2,
        cost=1 << 16,
    )
    peaks = [peak] + [to_z(peak, k) for k in (1, 2, 3)]
    pieces = list(inner_pieces(where, hidden, grad_out, peak, 1, pieces))
    *codes, step = call(
        encode_kernel,
        [bf16(4, 128, 256)] * 4 + [f32(128, 256)],
        (where, mine, other, *peaks, pieces[0]),
        [SMEM] + [VMEM] * 6 + [ANY],
        scratch=[pltpu.VMEM((16, 128, 256), jnp.float32)],
        cost=1 << 22,
    )
    parts = [codes[0]] + [to_x(codes[k], k) for k in (1, 2, 3)]
    pieces[1], pieces[2] = gate(codes[0], pieces[1], pieces[2])
    pieces[1], pieces[2] = to_y(pieces[1], 1), to_y(pieces[2], 2)
    sums = call(
        sum_x_kernel,
        [f32(128, 256)] + [bf16(128, 256)] * 3,
        (where, *parts),
        [SMEM] + [VMEM] * 4,
        cost=1 << 20,
    )
    (pieces[3],) = gate(sums[0], pieces[3])
    inner_keep, inner_give = call(
        sum_y_kernel,
        [f32(16, 8192), bf16(16, 8192)],
        (where, *pieces[:3], to_y(pieces[3], 3)),
        [SMEM] + [VMEM] * 4,
        cost=1 << 21,
    )
    parts = [sums[0]] + [to_z(sums[k], k) for k in (1, 2, 3)]
    anchor_next, momentum_next, params = call(
        update_kernel,
        [f32(128, 256), f32(128, 256), bf16(128, 256)],
        (*parts, step, anchor, momentum, pieces[1], pieces[2]),
        [VMEM] * 7 + [ANY] * 2,
        cost=1 << 19,
    )
    parts = [params] + [to_z(params, k) for k in (1, 2, 3)]
    (block,) = call(
        gather_z_kernel,
        [bf16(4, 128, 256)],
        (where, *parts, inner_give),
        [SMEM] + [VMEM] * 4 + [ANY],
    )
    far = [to_x(block, k) for k in (1, 2, 3)]
    twin = to_core(block)
    params_next = place(where, None, [(block, 0, 0), (twin, 1, 0)])
    twins = [to_core(a) for a in far]
    params_next = place(where, params_next, [(a, 0, k) for k, a in zip((1, 2, 3), far)])
    params_next = place(where, params_next, [(a, 1, k) for k, a in zip((1, 2, 3), twins)])
    grad_shard = (inner_keep + to_half(inner_give).astype(jnp.float32)).astype(jnp.bfloat16)
    return anchor_next, momentum_next, params_next, grad_shard[None]


def product_kernel(where, hidden, grad, after, *refs):
    o0, o1, o2, o3, left, whole = refs[-6:]

    @pl.when(pl.program_id(0) == 0)
    def _():
        left[...] = hidden[0].astype(jnp.float32).T.astype(jnp.bfloat16)

    whole[...] = jnp.dot(
        left[...], grad[0], preferred_element_type=jnp.float32
    ).astype(jnp.bfloat16)
    y = where[3]
    for k, out in enumerate((o0, o1, o2, o3)):
        for half in range(2):
            start = pl.multiple_of(half * 64 + lax.rem(y + k, 4) * 16, 16)
            out[half * 16 : half * 16 + 16, :] = whole[pl.ds(start, 16), :]


def sum_y_kernel(where, a0, a1, a2, a3, keep, give):
    half = where[4]
    for side, out in ((half, keep), (1 - half, give)):
        rows = pl.ds(pl.multiple_of(side * 16, 16), 16)
        parts = [a[rows, :].astype(jnp.float32) for a in (a0, a1, a2, a3)]
        out[...] = ((parts[0] + parts[1]) + (parts[2] + parts[3])).astype(out.dtype)


def inner_pieces(where, hidden, grad_out, after, part, given=()):
    tile = 1024
    steps = 8192 // tile // 2
    return pl.pallas_call(
        product_kernel,
        grid=(steps,),
        out_shape=[bf16(32, 8192)] * 4,
        in_specs=[
            SMEM,
            pl.BlockSpec((1, 384, 128), lambda i: (0, 0, 0)),
            pl.BlockSpec((1, 384, tile), lambda i: (0, 0, i + part * steps)),
            ANY,
        ]
        + [ANY] * len(given),
        out_specs=[pl.BlockSpec((32, tile), lambda i: (0, i + part * steps))] * 4,
        scratch_shapes=[
            pltpu.VMEM((128, 384), jnp.bfloat16),
            pltpu.VMEM((128, tile), jnp.bfloat16),
        ],
        input_output_aliases={4 + k: k for k in range(len(given))},
        cost_estimate=pl.CostEstimate(
            flops=128 * 384 * 8192, bytes_accessed=1 << 22, transcendentals=0
        ),
        compiler_params=pltpu.CompilerParams(vmem_limit_bytes=LIMIT),
    )(where, hidden, pltpu.with_memory_space_constraint(grad_out, pltpu.HBM), after, *given)


def on_device(pseudo_grad, anchor, momentum, hidden, grad_out):
    r, f = lax.axis_index("replica"), lax.axis_index("fsdp")
    where = jnp.stack([r & 1, (r >> 1) & 3, r >> 3, f & 3, f >> 2]).astype(jnp.int32)
    return both_steps(where, pseudo_grad, anchor, momentum, hidden, grad_out)


def solution(mesh):
    placed = (
        P("replica", "fsdp", None),
        P("fsdp", "replica"),
        P("fsdp", "replica"),
        P("replica", "fsdp", None),
        P("replica", "fsdp", None),
    )
    return jax.shard_map(
        on_device,
        mesh=mesh,
        in_specs=placed,
        out_specs=(
            P("fsdp", "replica"),
            P("fsdp", "replica"),
            P("fsdp", None),
            P("replica", "fsdp", None),
        ),
        check_vma=False,
    )
```

```python
import functools

import jax
import jax.numpy as jnp
from jax import lax
from jax.experimental import pallas as pl
from jax.experimental.pallas import tpu as pltpu
from jax.sharding import PartitionSpec as P

BLOCK = 128
EPSILON = 1e-06
TOP_EXPONENT = 6
OUTER_MOMENTUM = 0.9
OUTER_RATE = 0.7
LIMIT = 16 * 1024 * 1024

ANY = pl.BlockSpec(memory_space=pl.ANY)
VMEM = pl.BlockSpec(memory_space=pltpu.VMEM)
HBM = pl.BlockSpec(memory_space=pltpu.HBM)
SMEM = pl.BlockSpec(memory_space=pltpu.SMEM)


def replica_perm(move):
    pairs = []
    for z in range(4):
        for x in range(4):
            for c in range(2):
                to = move(z, x, c)
                pairs.append((z * 8 + x * 2 + c, to[0] * 8 + to[1] * 2 + to[2]))
    return pairs


def fsdp_perm(move):
    pairs = []
    for h in range(2):
        for y in range(4):
            to = move(h, y)
            pairs.append((h * 4 + y, to[0] * 4 + to[1]))
    return pairs


def to_core(a):
    return lax.ppermute(a, "replica", replica_perm(lambda z, x, c: (z, x, 1 - c)))


def to_x(a, k):
    return lax.ppermute(a, "replica", replica_perm(lambda z, x, c: (z, (x + k) % 4, c)))


def to_z(a, k):
    return lax.ppermute(a, "replica", replica_perm(lambda z, x, c: (z ^ k, x, c)))


def to_y(a, k):
    return lax.ppermute(a, "fsdp", fsdp_perm(lambda h, y: (h, (y + k) % 4)))


def to_half(a):
    return lax.ppermute(a, "fsdp", fsdp_perm(lambda h, y: (1 - h, y)))


def call(kernel, out, ins, specs, out_specs=None, scratch=(), cost=0, alias=None):
    return pl.pallas_call(
        kernel,
        out_shape=out,
        in_specs=specs,
        out_specs=out_specs if out_specs is not None else [VMEM] * len(out),
        scratch_shapes=list(scratch),
        input_output_aliases=alias or {},
        cost_estimate=pl.CostEstimate(flops=cost, bytes_accessed=cost, transcendentals=0),
        compiler_params=pltpu.CompilerParams(vmem_limit_bytes=LIMIT),
    )(*ins)


def gate_kernel(*refs):
    pass


def gate(after, *arrays):
    n = len(arrays)
    return call(
        gate_kernel,
        [jax.ShapeDtypeStruct(a.shape, a.dtype) for a in arrays],
        (*arrays, *after),
        [ANY] * (n + len(after)),
        [ANY] * n,
        cost=1 << 10,
        alias={i: i for i in range(n)},
    )


def bf16(*shape):
    return jax.ShapeDtypeStruct(shape, jnp.bfloat16)


def f32(*shape):
    return jax.ShapeDtypeStruct(shape, jnp.float32)


def split_kernel(where, grad, keep, give, keep_peak, give_peak, rows, tops, sems):
    core = where[0]

    def fetch(i):
        part = pl.ds(pl.multiple_of(i * 16, 16), 16)
        return pltpu.make_async_copy(grad.at[0, part, :], rows.at[part, :], sems.at[i])

    for i in range(8):
        fetch(i).start()
    lanes = lax.broadcasted_iota(jnp.int32, (16, 128), 1)

    def chunk(i, carry):
        fetch(i).wait()
        part = pl.ds(pl.multiple_of(i * 16, 16), 16)
        acc = jnp.zeros((16, 128), jnp.float32)
        for n in range(16):
            for k, (side, out) in enumerate(((core, keep), (1 - core, give))):
                start = pl.multiple_of(n * 512 + side * 256, 256)
                value = rows[part, pl.ds(start, 256)]
                out[n, part, :] = value
                size = jnp.abs(value)
                for b in range(2):
                    block = size[:, b * BLOCK : (b + 1) * BLOCK].astype(jnp.float32)
                    top = jnp.max(block, axis=1, keepdims=True)
                    acc = jnp.where(lanes == 32 * k + 2 * n + b, top, acc)
        tops[part, :] = acc
        return carry

    lax.fori_loop(0, 8, chunk, 0)
    flat = tops[...].T
    keep_peak[...] = flat[:32].astype(jnp.bfloat16)
    give_peak[...] = flat[32:64].astype(jnp.bfloat16)


def top_kernel(a0, a1, a2, a3, *rest):
    out = rest[-1]
    out[...] = jnp.maximum(jnp.maximum(a0[...], a1[...]), jnp.maximum(a2[...], a3[...]))


def scale_of(peak):
    bounded = peak + EPSILON
    scale = jnp.ones_like(bounded)
    for e in range(1, 26):
        scale = jnp.where(bounded <= 2.0 ** (TOP_EXPONENT - e), 2.0**e, scale)
    return scale


def encode_kernel(where, mine, other, p0, p1, p2, p3, after, o0, o1, o2, o3, step, scales):
    x, z = where[1], where[2]
    peak = jnp.maximum(
        jnp.maximum(p0[...].astype(jnp.float32), p1[...].astype(jnp.float32)),
        jnp.maximum(p2[...].astype(jnp.float32), p3[...].astype(jnp.float32)),
    )
    scale = scale_of(peak)
    wide = jnp.concatenate([scale, jnp.ones((96, 128), jnp.float32)], axis=0).T
    for n in range(32):
        scales[n // 2, :, (n % 2) * BLOCK : (n % 2 + 1) * BLOCK] = jnp.broadcast_to(
            wide[:, n : n + 1], (128, 128)
        )
    step[...] = 1.0 / (scales[z * 4 + x] * 32.0)
    for k, out in enumerate((o0, o1, o2, o3)):
        column = lax.rem(x + k, 4)
        for level in range(4):
            n = level * 4 + column
            s = scales[n]
            first = jnp.floor(mine[n].astype(jnp.float32) * s + 0.5)
            second = jnp.floor(other[n].astype(jnp.float32) * s + 0.5)
            out[level] = (first + second).astype(jnp.bfloat16)


def sum_x_kernel(where, a0, a1, a2, a3, o0, o1, o2, o3):
    z = where[2]
    for k, out in enumerate((o0, o1, o2, o3)):
        level = z ^ k
        parts = [a[level].astype(jnp.float32) for a in (a0, a1, a2, a3)]
        out[...] = (((parts[0] + parts[1]) + (parts[2] + parts[3]))).astype(out.dtype)


def update_kernel(a0, a1, a2, a3, step, anchor, momentum, anchor_out, momentum_out, params):
    parts = [a[...].astype(jnp.float32) for a in (a0, a1, a2, a3)]
    total = (parts[0] + parts[1]) + (parts[2] + parts[3])
    delta = total * step[...]
    fresh = OUTER_MOMENTUM * momentum[...] + delta
    moved = anchor[...] - OUTER_RATE * (delta + OUTER_MOMENTUM * fresh)
    momentum_out[...] = fresh
    anchor_out[...] = moved
    params[...] = moved.astype(jnp.bfloat16)


def gather_z_kernel(where, a0, a1, a2, a3, after, out):
    z = where[2]
    for k, a in enumerate((a0, a1, a2, a3)):
        out[z ^ k] = a[...]


def place_copies(sides, turns, where, blocks, out, sems):
    core, x = where[0], where[1]
    copies = []
    for block, side, turn in zip(blocks, sides, turns):
        column = lax.rem(x + 4 - turn, 4)
        half = core if side == 0 else 1 - core
        for level in range(4):
            start = pl.multiple_of((level * 4 + column) * 512 + half * 256, 256)
            copies.append(
                pltpu.make_async_copy(
                    block.at[level], out.at[:, pl.ds(start, 256)], sems.at[len(copies)]
                )
            )
    return copies


def place_kernel(sides, turns, where, *refs):
    copies = place_copies(sides, turns, where, refs[: len(sides)], refs[-2], refs[-1])
    for copy in copies:
        copy.start()
    for copy in copies:
        copy.wait()


def add_halves_kernel(keep, came, out, token):
    out[0] = (keep[...] + came[...].astype(jnp.float32)).astype(jnp.bfloat16)
    token[...] = jnp.zeros_like(token)


def place(where, out, items):
    blocks, sides, turns = zip(*items)
    given = [] if out is None else [out]
    return call(
        functools.partial(place_kernel, sides, turns),
        [bf16(128, 8192)],
        (where, *blocks, *given),
        [SMEM] + [VMEM] * len(blocks) + [HBM] * len(given),
        [HBM],
        scratch=[pltpu.SemaphoreType.DMA((4 * len(blocks),))],
        cost=1 << 18,
        alias={1 + len(blocks): 0} if given else None,
    )[0]


def both_steps(where, pseudo_grad, anchor, momentum, hidden, grad_out):
    mine, give, peak, other_peak = call(
        split_kernel,
        [bf16(16, 128, 256)] * 2 + [bf16(32, 128)] * 2,
        (where, pltpu.with_memory_space_constraint(pseudo_grad, pltpu.HBM)),
        [SMEM, HBM],
        scratch=[
            pltpu.VMEM((128, 8192), jnp.bfloat16),
            pltpu.VMEM((128, 128), jnp.float32),
            pltpu.SemaphoreType.DMA((8,)),
        ],
        cost=1 << 21,
    )
    peak = jnp.maximum(peak, to_core(other_peak))
    other = to_core(give)
    near = [to_x(peak, k) for k in (1, 2, 3)]
    pieces = inner_pieces(where, hidden, grad_out, peak, 0)
    (peak,) = call(
        top_kernel,
        [bf16(32, 128)],
        (peak, *near, other, pieces[0]),
        [VMEM] * 4 + [ANY] * 2,
        cost=1 << 16,
    )
    peaks = [peak] + [to_z(peak, k) for k in (1, 2, 3)]
    pieces = list(inner_pieces(where, hidden, grad_out, peak, 1, pieces))
    *codes, step = call(
        encode_kernel,
        [bf16(4, 128, 256)] * 4 + [f32(128, 256)],
        (where, mine, other, *peaks, pieces[0]),
        [SMEM] + [VMEM] * 6 + [ANY],
        scratch=[pltpu.VMEM((16, 128, 256), jnp.float32)],
        cost=1 << 22,
    )
    parts = [codes[0]] + [to_x(codes[k], k) for k in (1, 2, 3)]
    pieces[1], pieces[2] = gate((codes[0],), pieces[1], pieces[2])
    pieces[1], pieces[2] = to_y(pieces[1], 1), to_y(pieces[2], 2)
    sums = call(
        sum_x_kernel,
        [f32(128, 256)] + [bf16(128, 256)] * 3,
        (where, *parts),
        [SMEM] + [VMEM] * 4,
        cost=1 << 20,
    )
    (pieces[3],) = gate((sums[0],), pieces[3])
    inner_keep, inner_give = call(
        sum_y_kernel,
        [f32(16, 8192), bf16(16, 8192)],
        (where, *pieces[:3], to_y(pieces[3], 3)),
        [SMEM] + [VMEM] * 4,
        cost=1 << 21,
    )
    parts = [sums[0]] + [to_z(sums[k], k) for k in (1, 2, 3)]
    anchor_next, momentum_next, params = call(
        update_kernel,
        [f32(128, 256), f32(128, 256), bf16(128, 256)],
        (*parts, step, anchor, momentum),
        [VMEM] * 7,
        cost=1 << 19,
    )
    parts = [params] + [to_z(params, k) for k in (1, 2, 3)]
    (block,) = call(
        gather_z_kernel,
        [bf16(4, 128, 256)],
        (where, *parts, inner_give),
        [SMEM] + [VMEM] * 4 + [ANY],
    )
    far = [to_x(block, k) for k in (1, 2, 3)]
    twin = to_core(block)
    grad_shard, token = call(
        add_halves_kernel,
        [bf16(1, 16, 8192), f32(8, 128)],
        (inner_keep, to_half(inner_give)),
        [VMEM] * 2,
        cost=1 << 20,
    )
    far = gate((token,), *far)
    twins = [to_core(a) for a in far]
    params_next = place(
        where, None, [(a, 0, k) for k, a in enumerate([block, *far])] + [(twin, 1, 0)]
    )
    params_next = place(where, params_next, [(a, 1, k) for k, a in zip((1, 2, 3), twins)])
    return anchor_next, momentum_next, params_next, grad_shard


def product_kernel(where, hidden, grad, after, *refs):
    o0, o1, o2, o3, left, whole = refs[-6:]

    @pl.when(pl.program_id(0) == 0)
    def _():
        left[...] = hidden[0].astype(jnp.float32).T.astype(jnp.bfloat16)

    whole[...] = jnp.dot(
        left[...], grad[0], preferred_element_type=jnp.float32
    ).astype(jnp.bfloat16)
    y = where[3]
    for k, out in enumerate((o0, o1, o2, o3)):
        for half in range(2):
            start = pl.multiple_of(half * 64 + lax.rem(y + k, 4) * 16, 16)
            out[half * 16 : half * 16 + 16, :] = whole[pl.ds(start, 16), :]


def sum_y_kernel(where, a0, a1, a2, a3, keep, give):
    half = where[4]
    for side, out in ((half, keep), (1 - half, give)):
        rows = pl.ds(pl.multiple_of(side * 16, 16), 16)
        parts = [a[rows, :].astype(jnp.float32) for a in (a0, a1, a2, a3)]
        out[...] = ((parts[0] + parts[1]) + (parts[2] + parts[3])).astype(out.dtype)


def inner_pieces(where, hidden, grad_out, after, part, given=()):
    tile = 1024
    steps = 8192 // tile // 2
    return pl.pallas_call(
        product_kernel,
        grid=(steps,),
        out_shape=[bf16(32, 8192)] * 4,
        in_specs=[
            SMEM,
            pl.BlockSpec((1, 384, 128), lambda i: (0, 0, 0)),
            pl.BlockSpec((1, 384, tile), lambda i: (0, 0, i + part * steps)),
            ANY,
        ]
        + [ANY] * len(given),
        out_specs=[pl.BlockSpec((32, tile), lambda i: (0, i + part * steps))] * 4,
        scratch_shapes=[
            pltpu.VMEM((128, 384), jnp.bfloat16),
            pltpu.VMEM((128, tile), jnp.bfloat16),
        ],
        input_output_aliases={4 + k: k for k in range(len(given))},
        cost_estimate=pl.CostEstimate(
            flops=128 * 384 * 8192, bytes_accessed=1 << 22, transcendentals=0
        ),
        compiler_params=pltpu.CompilerParams(vmem_limit_bytes=LIMIT),
    )(where, hidden, pltpu.with_memory_space_constraint(grad_out, pltpu.HBM), after, *given)


def on_device(pseudo_grad, anchor, momentum, hidden, grad_out):
    r, f = lax.axis_index("replica"), lax.axis_index("fsdp")
    where = jnp.stack([r & 1, (r >> 1) & 3, r >> 3, f & 3, f >> 2]).astype(jnp.int32)
    return both_steps(where, pseudo_grad, anchor, momentum, hidden, grad_out)


def solution(mesh):
    placed = (
        P("replica", "fsdp", None),
        P("fsdp", "replica"),
        P("fsdp", "replica"),
        P("replica", "fsdp", None),
        P("replica", "fsdp", None),
    )
    return jax.shard_map(
        on_device,
        mesh=mesh,
        in_specs=placed,
        out_specs=(
            P("fsdp", "replica"),
            P("fsdp", "replica"),
            P("fsdp", None),
            P("replica", "fsdp", None),
        ),
        check_vma=False,
    )
```

```python
import functools

import jax
import jax.numpy as jnp
from jax import lax
from jax.experimental import pallas as pl
from jax.experimental.pallas import tpu as pltpu
from jax.sharding import PartitionSpec as P

BLOCK = 128
EPSILON = 1e-06
TOP_EXPONENT = 6
OUTER_MOMENTUM = 0.9
OUTER_RATE = 0.7
LIMIT = 16 * 1024 * 1024

ANY = pl.BlockSpec(memory_space=pl.ANY)
VMEM = pl.BlockSpec(memory_space=pltpu.VMEM)
HBM = pl.BlockSpec(memory_space=pltpu.HBM)
SMEM = pl.BlockSpec(memory_space=pltpu.SMEM)


def replica_perm(move):
    pairs = []
    for z in range(4):
        for x in range(4):
            for c in range(2):
                to = move(z, x, c)
                pairs.append((z * 8 + x * 2 + c, to[0] * 8 + to[1] * 2 + to[2]))
    return pairs


def fsdp_perm(move):
    pairs = []
    for h in range(2):
        for y in range(4):
            to = move(h, y)
            pairs.append((h * 4 + y, to[0] * 4 + to[1]))
    return pairs


def to_core(a):
    return lax.ppermute(a, "replica", replica_perm(lambda z, x, c: (z, x, 1 - c)))


def to_x(a, k):
    return lax.ppermute(a, "replica", replica_perm(lambda z, x, c: (z, (x + k) % 4, c)))


def to_z(a, k):
    return lax.ppermute(a, "replica", replica_perm(lambda z, x, c: (z ^ k, x, c)))


def to_y(a, k):
    return lax.ppermute(a, "fsdp", fsdp_perm(lambda h, y: (h, (y + k) % 4)))


def to_half(a):
    return lax.ppermute(a, "fsdp", fsdp_perm(lambda h, y: (1 - h, y)))


def call(kernel, out, ins, specs, out_specs=None, scratch=(), cost=0, alias=None):
    return pl.pallas_call(
        kernel,
        out_shape=out,
        in_specs=specs,
        out_specs=out_specs if out_specs is not None else [VMEM] * len(out),
        scratch_shapes=list(scratch),
        input_output_aliases=alias or {},
        cost_estimate=pl.CostEstimate(flops=cost, bytes_accessed=cost, transcendentals=0),
        compiler_params=pltpu.CompilerParams(vmem_limit_bytes=LIMIT),
    )(*ins)


def gate_kernel(*refs):
    pass


def gate(after, *arrays):
    n = len(arrays)
    return call(
        gate_kernel,
        [jax.ShapeDtypeStruct(a.shape, a.dtype) for a in arrays],
        (*arrays, *after),
        [ANY] * (n + len(after)),
        [ANY] * n,
        cost=1 << 10,
        alias={i: i for i in range(n)},
    )


def bf16(*shape):
    return jax.ShapeDtypeStruct(shape, jnp.bfloat16)


def f32(*shape):
    return jax.ShapeDtypeStruct(shape, jnp.float32)


def split_kernel(where, grad, keep, give, keep_peak, give_peak, rows, tops, sems):
    core = where[0]

    def fetch(i):
        part = pl.ds(pl.multiple_of(i * 16, 16), 16)
        return pltpu.make_async_copy(grad.at[0, part, :], rows.at[part, :], sems.at[i])

    for i in range(8):
        fetch(i).start()
    lanes = lax.broadcasted_iota(jnp.int32, (16, 128), 1)

    def chunk(i, carry):
        fetch(i).wait()
        part = pl.ds(pl.multiple_of(i * 16, 16), 16)
        acc = jnp.zeros((16, 128), jnp.float32)
        for n in range(16):
            for k, (side, out) in enumerate(((core, keep), (1 - core, give))):
                start = pl.multiple_of(n * 512 + side * 256, 256)
                value = rows[part, pl.ds(start, 256)]
                out[n, part, :] = value
                size = jnp.abs(value)
                for b in range(2):
                    block = size[:, b * BLOCK : (b + 1) * BLOCK].astype(jnp.float32)
                    top = jnp.max(block, axis=1, keepdims=True)
                    acc = jnp.where(lanes == 32 * k + 2 * n + b, top, acc)
        tops[part, :] = acc
        return carry

    lax.fori_loop(0, 8, chunk, 0)
    flat = tops[...].T
    keep_peak[...] = flat[:32].astype(jnp.bfloat16)
    give_peak[...] = flat[32:64].astype(jnp.bfloat16)


def top_kernel(a0, a1, a2, a3, *rest):
    out = rest[-1]
    out[...] = jnp.maximum(jnp.maximum(a0[...], a1[...]), jnp.maximum(a2[...], a3[...]))


def scale_of(peak):
    bounded = peak + EPSILON
    scale = jnp.ones_like(bounded)
    for e in range(1, 26):
        scale = jnp.where(bounded <= 2.0 ** (TOP_EXPONENT - e), 2.0**e, scale)
    return scale


def encode_kernel(where, mine, other, p0, p1, p2, p3, after, o0, o1, o2, o3, step, scales):
    x, z = where[1], where[2]
    peak = jnp.maximum(
        jnp.maximum(p0[...].astype(jnp.float32), p1[...].astype(jnp.float32)),
        jnp.maximum(p2[...].astype(jnp.float32), p3[...].astype(jnp.float32)),
    )
    scale = scale_of(peak)
    wide = jnp.concatenate([scale, jnp.ones((96, 128), jnp.float32)], axis=0).T
    for n in range(32):
        scales[n // 2, :, (n % 2) * BLOCK : (n % 2 + 1) * BLOCK] = jnp.broadcast_to(
            wide[:, n : n + 1], (128, 128)
        )
    step[...] = 1.0 / (scales[z * 4 + x] * 32.0)
    for k, out in enumerate((o0, o1, o2, o3)):
        column = lax.rem(x + k, 4)
        for level in range(4):
            n = level * 4 + column
            s = scales[n]
            first = jnp.floor(mine[n].astype(jnp.float32) * s + 0.5)
            second = jnp.floor(other[n].astype(jnp.float32) * s + 0.5)
            out[level] = (first + second).astype(jnp.bfloat16)


def sum_x_kernel(where, a0, a1, a2, a3, o0, o1, o2, o3):
    z = where[2]
    for k, out in enumerate((o0, o1, o2, o3)):
        level = z ^ k
        parts = [a[level].astype(jnp.float32) for a in (a0, a1, a2, a3)]
        out[...] = (((parts[0] + parts[1]) + (parts[2] + parts[3]))).astype(out.dtype)


def update_kernel(a0, a1, a2, a3, step, anchor, momentum, after1, after2, anchor_out, momentum_out, params):
    parts = [a[...].astype(jnp.float32) for a in (a0, a1, a2, a3)]
    total = (parts[0] + parts[1]) + (parts[2] + parts[3])
    delta = total * step[...]
    fresh = OUTER_MOMENTUM * momentum[...] + delta
    moved = anchor[...] - OUTER_RATE * (delta + OUTER_MOMENTUM * fresh)
    momentum_out[...] = fresh
    anchor_out[...] = moved
    params[...] = moved.astype(jnp.bfloat16)


def gather_z_kernel(where, a0, a1, a2, a3, after, out):
    z = where[2]
    for k, a in enumerate((a0, a1, a2, a3)):
        out[z ^ k] = a[...]


def place_copies(sides, turns, where, blocks, out, sems):
    core, x = where[0], where[1]
    copies = []
    for block, side, turn in zip(blocks, sides, turns):
        column = lax.rem(x + 4 - turn, 4)
        half = core if side == 0 else 1 - core
        for level in range(4):
            start = pl.multiple_of((level * 4 + column) * 512 + half * 256, 256)
            copies.append(
                pltpu.make_async_copy(
                    block.at[level], out.at[:, pl.ds(start, 256)], sems.at[len(copies)]
                )
            )
    return copies


def place_kernel(sides, turns, where, *refs):
    copies = place_copies(sides, turns, where, refs[: len(sides)], refs[-2], refs[-1])
    for copy in copies:
        copy.start()
    for copy in copies:
        copy.wait()


def add_halves_kernel(keep, came, out, token):
    out[0] = (keep[...] + came[...].astype(jnp.float32)).astype(jnp.bfloat16)
    token[...] = jnp.zeros_like(token)


def place(where, out, items):
    blocks, sides, turns = zip(*items)
    given = [] if out is None else [out]
    return call(
        functools.partial(place_kernel, sides, turns),
        [bf16(128, 8192)],
        (where, *blocks, *given),
        [SMEM] + [VMEM] * len(blocks) + [HBM] * len(given),
        [HBM],
        scratch=[pltpu.SemaphoreType.DMA((4 * len(blocks),))],
        cost=1 << 18,
        alias={1 + len(blocks): 0} if given else None,
    )[0]


def both_steps(where, pseudo_grad, anchor, momentum, hidden, grad_out):
    mine, give, peak, other_peak = call(
        split_kernel,
        [bf16(16, 128, 256)] * 2 + [bf16(32, 128)] * 2,
        (where, pltpu.with_memory_space_constraint(pseudo_grad, pltpu.HBM)),
        [SMEM, HBM],
        scratch=[
            pltpu.VMEM((128, 8192), jnp.bfloat16),
            pltpu.VMEM((128, 128), jnp.float32),
            pltpu.SemaphoreType.DMA((8,)),
        ],
        cost=1 << 21,
    )
    peak = jnp.maximum(peak, to_core(other_peak))
    (give,) = gate((peak,), give)
    other = to_core(give)
    near = [to_x(peak, k) for k in (1, 2, 3)]
    pieces = inner_pieces(where, hidden, grad_out, peak, 0)
    (peak,) = call(
        top_kernel,
        [bf16(32, 128)],
        (peak, *near, other, pieces[0]),
        [VMEM] * 4 + [ANY] * 2,
        cost=1 << 16,
    )
    peaks = [peak] + [to_z(peak, k) for k in (1, 2, 3)]
    pieces = list(inner_pieces(where, hidden, grad_out, peak, 1, pieces))
    *codes, step = call(
        encode_kernel,
        [bf16(4, 128, 256)] * 4 + [f32(128, 256)],
        (where, mine, other, *peaks, pieces[0]),
        [SMEM] + [VMEM] * 6 + [ANY],
        scratch=[pltpu.VMEM((16, 128, 256), jnp.float32)],
        cost=1 << 22,
    )
    parts = [codes[0]] + [to_x(codes[k], k) for k in (1, 2, 3)]
    pieces[1], pieces[2] = gate((codes[0],), pieces[1], pieces[2])
    pieces[1], pieces[2] = to_y(pieces[1], 1), to_y(pieces[2], 2)
    sums = call(
        sum_x_kernel,
        [f32(128, 256)] + [bf16(128, 256)] * 3,
        (where, *parts),
        [SMEM] + [VMEM] * 4,
        cost=1 << 31,
    )
    (pieces[3],) = gate((sums[0],), pieces[3])
    inner_keep, inner_give = call(
        sum_y_kernel,
        [f32(16, 8192), bf16(16, 8192)],
        (where, *pieces[:3], to_y(pieces[3], 3)),
        [SMEM] + [VMEM] * 4,
        cost=1 << 21,
    )
    parts = [sums[0]] + [to_z(sums[k], k) for k in (1, 2, 3)]
    anchor_next, momentum_next, params = call(
        update_kernel,
        [f32(128, 256), f32(128, 256), bf16(128, 256)],
        (*parts, step, anchor, momentum, pieces[1], pieces[2]),
        [VMEM] * 7 + [ANY] * 2,
        cost=1 << 32,
    )
    parts = [params] + [to_z(params, k) for k in (1, 2, 3)]
    (block,) = call(
        gather_z_kernel,
        [bf16(4, 128, 256)],
        (where, *parts, inner_give),
        [SMEM] + [VMEM] * 4 + [ANY],
    )
    far = [to_x(block, k) for k in (1, 2, 3)]
    twin = to_core(block)
    grad_shard, token = call(
        add_halves_kernel,
        [bf16(1, 16, 8192), f32(8, 128)],
        (inner_keep, to_half(inner_give)),
        [VMEM] * 2,
        cost=1 << 20,
    )
    far = gate((token,), *far)
    twins = [to_core(a) for a in far]
    params_next = place(
        where, None, [(a, 0, k) for k, a in enumerate([block, *far])] + [(twin, 1, 0)]
    )
    params_next = place(where, params_next, [(a, 1, k) for k, a in zip((1, 2, 3), twins)])
    return anchor_next, momentum_next, params_next, grad_shard


def product_kernel(where, hidden, grad, after, *refs):
    o0, o1, o2, o3, left, whole = refs[-6:]

    @pl.when(pl.program_id(0) == 0)
    def _():
        left[...] = hidden[0].astype(jnp.float32).T.astype(jnp.bfloat16)

    whole[...] = jnp.dot(
        left[...], grad[0], preferred_element_type=jnp.float32
    ).astype(jnp.bfloat16)
    y = where[3]
    for k, out in enumerate((o0, o1, o2, o3)):
        for half in range(2):
            start = pl.multiple_of(half * 64 + lax.rem(y + k, 4) * 16, 16)
            out[half * 16 : half * 16 + 16, :] = whole[pl.ds(start, 16), :]


def sum_y_kernel(where, a0, a1, a2, a3, keep, give):
    half = where[4]
    for side, out in ((half, keep), (1 - half, give)):
        rows = pl.ds(pl.multiple_of(side * 16, 16), 16)
        parts = [a[rows, :].astype(jnp.float32) for a in (a0, a1, a2, a3)]
        out[...] = ((parts[0] + parts[1]) + (parts[2] + parts[3])).astype(out.dtype)


def inner_pieces(where, hidden, grad_out, after, part, given=()):
    tile = 1024
    steps = 8192 // tile // 2
    return pl.pallas_call(
        product_kernel,
        grid=(steps,),
        out_shape=[bf16(32, 8192)] * 4,
        in_specs=[
            SMEM,
            pl.BlockSpec((1, 384, 128), lambda i: (0, 0, 0)),
            pl.BlockSpec((1, 384, tile), lambda i: (0, 0, i + part * steps)),
            ANY,
        ]
        + [ANY] * len(given),
        out_specs=[pl.BlockSpec((32, tile), lambda i: (0, i + part * steps))] * 4,
        scratch_shapes=[
            pltpu.VMEM((128, 384), jnp.bfloat16),
            pltpu.VMEM((128, tile), jnp.bfloat16),
        ],
        input_output_aliases={4 + k: k for k in range(len(given))},
        cost_estimate=pl.CostEstimate(
            flops=128 * 384 * 8192, bytes_accessed=1 << 22, transcendentals=0
        ),
        compiler_params=pltpu.CompilerParams(vmem_limit_bytes=LIMIT),
    )(where, hidden, pltpu.with_memory_space_constraint(grad_out, pltpu.HBM), after, *given)


def on_device(pseudo_grad, anchor, momentum, hidden, grad_out):
    r, f = lax.axis_index("replica"), lax.axis_index("fsdp")
    where = jnp.stack([r & 1, (r >> 1) & 3, r >> 3, f & 3, f >> 2]).astype(jnp.int32)
    return both_steps(where, pseudo_grad, anchor, momentum, hidden, grad_out)


def solution(mesh):
    placed = (
        P("replica", "fsdp", None),
        P("fsdp", "replica"),
        P("fsdp", "replica"),
        P("replica", "fsdp", None),
        P("replica", "fsdp", None),
    )
    return jax.shard_map(
        on_device,
        mesh=mesh,
        in_specs=placed,
        out_specs=(
            P("fsdp", "replica"),
            P("fsdp", "replica"),
            P("fsdp", None),
            P("replica", "fsdp", None),
        ),
        check_vma=False,
    )
```

```python
import functools

import jax
import jax.numpy as jnp
from jax import lax
from jax.experimental import pallas as pl
from jax.experimental.pallas import tpu as pltpu
from jax.sharding import PartitionSpec as P

BLOCK = 128
EPSILON = 1e-06
TOP_EXPONENT = 6
OUTER_MOMENTUM = 0.9
OUTER_RATE = 0.7
LIMIT = 16 * 1024 * 1024

ANY = pl.BlockSpec(memory_space=pl.ANY)
VMEM = pl.BlockSpec(memory_space=pltpu.VMEM)
HBM = pl.BlockSpec(memory_space=pltpu.HBM)
SMEM = pl.BlockSpec(memory_space=pltpu.SMEM)


def replica_perm(move):
    pairs = []
    for z in range(4):
        for x in range(4):
            for c in range(2):
                to = move(z, x, c)
                pairs.append((z * 8 + x * 2 + c, to[0] * 8 + to[1] * 2 + to[2]))
    return pairs


def fsdp_perm(move):
    pairs = []
    for h in range(2):
        for y in range(4):
            to = move(h, y)
            pairs.append((h * 4 + y, to[0] * 4 + to[1]))
    return pairs


def to_core(a):
    return lax.ppermute(a, "replica", replica_perm(lambda z, x, c: (z, x, 1 - c)))


def to_x(a, k):
    return lax.ppermute(a, "replica", replica_perm(lambda z, x, c: (z, (x + k) % 4, c)))


def to_z(a, k):
    return lax.ppermute(a, "replica", replica_perm(lambda z, x, c: (z ^ k, x, c)))


def to_y(a, k):
    return lax.ppermute(a, "fsdp", fsdp_perm(lambda h, y: (h, (y + k) % 4)))


def to_half(a):
    return lax.ppermute(a, "fsdp", fsdp_perm(lambda h, y: (1 - h, y)))


def call(kernel, out, ins, specs, out_specs=None, scratch=(), cost=0, alias=None):
    return pl.pallas_call(
        kernel,
        out_shape=out,
        in_specs=specs,
        out_specs=out_specs if out_specs is not None else [VMEM] * len(out),
        scratch_shapes=list(scratch),
        input_output_aliases=alias or {},
        cost_estimate=pl.CostEstimate(flops=cost, bytes_accessed=cost, transcendentals=0),
        compiler_params=pltpu.CompilerParams(vmem_limit_bytes=LIMIT),
    )(*ins)


def gate_kernel(*refs):
    pass


def gate(after, *arrays):
    n = len(arrays)
    return call(
        gate_kernel,
        [jax.ShapeDtypeStruct(a.shape, a.dtype) for a in arrays],
        (*arrays, *after),
        [ANY] * (n + len(after)),
        [ANY] * n,
        cost=1 << 10,
        alias={i: i for i in range(n)},
    )


def bf16(*shape):
    return jax.ShapeDtypeStruct(shape, jnp.bfloat16)


def f32(*shape):
    return jax.ShapeDtypeStruct(shape, jnp.float32)


def split_kernel(where, grad, keep, give, keep_peak, give_peak, rows, tops, sems):
    core = where[0]

    def fetch(i):
        part = pl.ds(pl.multiple_of(i * 32, 32), 32)
        return pltpu.make_async_copy(grad.at[0, part, :], rows.at[part, :], sems.at[i])

    for i in range(4):
        fetch(i).start()
    lanes = lax.broadcasted_iota(jnp.int32, (32, 128), 1)

    def chunk(i, carry):
        fetch(i).wait()
        part = pl.ds(pl.multiple_of(i * 32, 32), 32)
        acc = jnp.zeros((32, 128), jnp.float32)
        for n in range(16):
            for k, (side, out) in enumerate(((core, keep), (1 - core, give))):
                start = pl.multiple_of(n * 512 + side * 256, 256)
                value = rows[part, pl.ds(start, 256)]
                out[n, part, :] = value
                size = jnp.abs(value)
                for b in range(2):
                    block = size[:, b * BLOCK : (b + 1) * BLOCK].astype(jnp.float32)
                    top = jnp.max(block, axis=1, keepdims=True)
                    acc = jnp.where(lanes == 32 * k + 2 * n + b, top, acc)
        tops[part, :] = acc
        return carry

    lax.fori_loop(0, 4, chunk, 0)
    flat = tops[...].T
    keep_peak[...] = flat[:32].astype(jnp.bfloat16)
    give_peak[...] = flat[32:64].astype(jnp.bfloat16)


def top_kernel(a0, a1, a2, a3, *rest):
    out = rest[-1]
    out[...] = jnp.maximum(jnp.maximum(a0[...], a1[...]), jnp.maximum(a2[...], a3[...]))


def scale_of(peak):
    bounded = peak + EPSILON
    scale = jnp.ones_like(bounded)
    for e in range(1, 26):
        scale = jnp.where(bounded <= 2.0 ** (TOP_EXPONENT - e), 2.0**e, scale)
    return scale


def encode_kernel(where, mine, other, p0, p1, p2, p3, after, o0, o1, o2, o3, step, scales):
    x, z = where[1], where[2]
    peak = jnp.maximum(
        jnp.maximum(p0[...].astype(jnp.float32), p1[...].astype(jnp.float32)),
        jnp.maximum(p2[...].astype(jnp.float32), p3[...].astype(jnp.float32)),
    )
    scale = scale_of(peak)
    wide = jnp.concatenate([scale, jnp.ones((96, 128), jnp.float32)], axis=0).T
    for n in range(32):
        scales[n // 2, :, (n % 2) * BLOCK : (n % 2 + 1) * BLOCK] = jnp.broadcast_to(
            wide[:, n : n + 1], (128, 128)
        )
    step[...] = 1.0 / (scales[z * 4 + x] * 32.0)
    for k, out in enumerate((o0, o1, o2, o3)):
        column = lax.rem(x + k, 4)
        for level in range(4):
            n = level * 4 + column
            s = scales[n]
            first = jnp.floor(mine[n].astype(jnp.float32) * s + 0.5)
            second = jnp.floor(other[n].astype(jnp.float32) * s + 0.5)
            out[level] = (first + second).astype(jnp.bfloat16)


def sum_x_kernel(where, a0, a1, a2, a3, o0, o1, o2, o3):
    z = where[2]
    for k, out in enumerate((o0, o1, o2, o3)):
        level = z ^ k
        parts = [a[level].astype(jnp.float32) for a in (a0, a1, a2, a3)]
        out[...] = (((parts[0] + parts[1]) + (parts[2] + parts[3]))).astype(out.dtype)


def update_kernel(a0, a1, a2, a3, step, anchor, momentum, after1, after2, anchor_out, momentum_out, params):
    parts = [a[...].astype(jnp.float32) for a in (a0, a1, a2, a3)]
    total = (parts[0] + parts[1]) + (parts[2] + parts[3])
    delta = total * step[...]
    fresh = OUTER_MOMENTUM * momentum[...] + delta
    moved = anchor[...] - OUTER_RATE * (delta + OUTER_MOMENTUM * fresh)
    momentum_out[...] = fresh
    anchor_out[...] = moved
    params[...] = moved.astype(jnp.bfloat16)


def gather_z_kernel(where, a0, a1, a2, a3, after, out):
    z = where[2]
    for k, a in enumerate((a0, a1, a2, a3)):
        out[z ^ k] = a[...]


def place_copies(sides, turns, where, blocks, out, sems):
    core, x = where[0], where[1]
    copies = []
    for block, side, turn in zip(blocks, sides, turns):
        column = lax.rem(x + 4 - turn, 4)
        half = core if side == 0 else 1 - core
        for level in range(4):
            start = pl.multiple_of((level * 4 + column) * 512 + half * 256, 256)
            copies.append(
                pltpu.make_async_copy(
                    block.at[level], out.at[:, pl.ds(start, 256)], sems.at[len(copies)]
                )
            )
    return copies


def place_kernel(sides, turns, where, *refs):
    copies = place_copies(sides, turns, where, refs[: len(sides)], refs[-2], refs[-1])
    for copy in copies:
        copy.start()
    for copy in copies:
        copy.wait()


def add_halves_kernel(keep, came, out, token):
    out[0] = (keep[...] + came[...].astype(jnp.float32)).astype(jnp.bfloat16)
    token[...] = jnp.zeros_like(token)


def place(where, out, items):
    blocks, sides, turns = zip(*items)
    given = [] if out is None else [out]
    return call(
        functools.partial(place_kernel, sides, turns),
        [bf16(128, 8192)],
        (where, *blocks, *given),
        [SMEM] + [VMEM] * len(blocks) + [HBM] * len(given),
        [HBM],
        scratch=[pltpu.SemaphoreType.DMA((4 * len(blocks),))],
        cost=1 << 18,
        alias={1 + len(blocks): 0} if given else None,
    )[0]


def both_steps(where, pseudo_grad, anchor, momentum, hidden, grad_out):
    mine, give, peak, other_peak = call(
        split_kernel,
        [bf16(16, 128, 256)] * 2 + [bf16(32, 128)] * 2,
        (where, pltpu.with_memory_space_constraint(pseudo_grad, pltpu.HBM)),
        [SMEM, HBM],
        scratch=[
            pltpu.VMEM((128, 8192), jnp.bfloat16),
            pltpu.VMEM((128, 128), jnp.float32),
            pltpu.SemaphoreType.DMA((4,)),
        ],
        cost=1 << 21,
    )
    peak = jnp.maximum(peak, to_core(other_peak))
    (give,) = gate((peak,), give)
    other = to_core(give)
    near = [to_x(peak, k) for k in (1, 2, 3)]
    pieces = inner_pieces(where, hidden, grad_out, peak, 0)
    (peak,) = call(
        top_kernel,
        [bf16(32, 128)],
        (peak, *near, other, pieces[0]),
        [VMEM] * 4 + [ANY] * 2,
        cost=1 << 16,
    )
    peaks = [peak] + [to_z(peak, k) for k in (1, 2, 3)]
    pieces = list(inner_pieces(where, hidden, grad_out, peak, 1, pieces))
    *codes, step = call(
        encode_kernel,
        [bf16(4, 128, 256)] * 4 + [f32(128, 256)],
        (where, mine, other, *peaks, pieces[0]),
        [SMEM] + [VMEM] * 6 + [ANY],
        scratch=[pltpu.VMEM((16, 128, 256), jnp.float32)],
        cost=1 << 22,
    )
    parts = [codes[0]] + [to_x(codes[k], k) for k in (1, 2, 3)]
    pieces[1], pieces[3] = gate((codes[0],), pieces[1], pieces[3])
    pieces[1], pieces[3] = to_y(pieces[1], 1), to_y(pieces[3], 3)
    sums = call(
        sum_x_kernel,
        [f32(128, 256)] + [bf16(128, 256)] * 3,
        (where, *parts),
        [SMEM] + [VMEM] * 4,
        cost=1 << 31,
    )
    (pieces[2],) = gate((sums[0],), pieces[2])
    inner_keep, inner_give = call(
        sum_y_kernel,
        [f32(16, 8192), bf16(16, 8192)],
        (where, pieces[0], pieces[1], to_y(pieces[2], 2), pieces[3]),
        [SMEM] + [VMEM] * 4,
        cost=1 << 21,
    )
    parts = [sums[0]] + [to_z(sums[k], k) for k in (1, 2, 3)]
    anchor_next, momentum_next, params = call(
        update_kernel,
        [f32(128, 256), f32(128, 256), bf16(128, 256)],
        (*parts, step, anchor, momentum, pieces[1], pieces[3]),
        [VMEM] * 7 + [ANY] * 2,
        cost=1 << 32,
    )
    parts = [params] + [to_z(params, k) for k in (1, 2, 3)]
    (block,) = call(
        gather_z_kernel,
        [bf16(4, 128, 256)],
        (where, *parts, inner_give),
        [SMEM] + [VMEM] * 4 + [ANY],
    )
    far = [to_x(block, k) for k in (1, 2, 3)]
    twin = to_core(block)
    grad_shard, token = call(
        add_halves_kernel,
        [bf16(1, 16, 8192), f32(8, 128)],
        (inner_keep, to_half(inner_give)),
        [VMEM] * 2,
        cost=1 << 20,
    )
    far = gate((token,), *far)
    twins = [to_core(a) for a in far]
    params_next = place(
        where, None, [(a, 0, k) for k, a in enumerate([block, *far])] + [(twin, 1, 0)]
    )
    params_next = place(where, params_next, [(a, 1, k) for k, a in zip((1, 2, 3), twins)])
    return anchor_next, momentum_next, params_next, grad_shard


def product_kernel(where, hidden, grad, after, *refs):
    o0, o1, o2, o3, left, whole = refs[-6:]

    @pl.when(pl.program_id(0) == 0)
    def _():
        left[...] = hidden[0].astype(jnp.float32).T.astype(jnp.bfloat16)

    whole[...] = jnp.dot(
        left[...], grad[0], preferred_element_type=jnp.float32
    ).astype(jnp.bfloat16)
    y = where[3]
    for k, out in enumerate((o0, o1, o2, o3)):
        for half in range(2):
            start = pl.multiple_of(half * 64 + lax.rem(y + k, 4) * 16, 16)
            out[half * 16 : half * 16 + 16, :] = whole[pl.ds(start, 16), :]


def sum_y_kernel(where, a0, a1, a2, a3, keep, give):
    half = where[4]
    for side, out in ((half, keep), (1 - half, give)):
        rows = pl.ds(pl.multiple_of(side * 16, 16), 16)
        parts = [a[rows, :].astype(jnp.float32) for a in (a0, a1, a2, a3)]
        out[...] = ((parts[0] + parts[1]) + (parts[2] + parts[3])).astype(out.dtype)


def inner_pieces(where, hidden, grad_out, after, part, given=()):
    tile = 2048
    steps = 8192 // tile // 2
    return pl.pallas_call(
        product_kernel,
        grid=(steps,),
        out_shape=[bf16(32, 8192)] * 4,
        in_specs=[
            SMEM,
            pl.BlockSpec((1, 384, 128), lambda i: (0, 0, 0)),
            pl.BlockSpec((1, 384, tile), lambda i: (0, 0, i + part * steps)),
            ANY,
        ]
        + [ANY] * len(given),
        out_specs=[pl.BlockSpec((32, tile), lambda i: (0, i + part * steps))] * 4,
        scratch_shapes=[
            pltpu.VMEM((128, 384), jnp.bfloat16),
            pltpu.VMEM((128, tile), jnp.bfloat16),
        ],
        input_output_aliases={4 + k: k for k in range(len(given))},
        cost_estimate=pl.CostEstimate(
            flops=128 * 384 * 8192, bytes_accessed=1 << 22, transcendentals=0
        ),
        compiler_params=pltpu.CompilerParams(vmem_limit_bytes=LIMIT),
    )(where, hidden, pltpu.with_memory_space_constraint(grad_out, pltpu.HBM), after, *given)


def on_device(pseudo_grad, anchor, momentum, hidden, grad_out):
    r, f = lax.axis_index("replica"), lax.axis_index("fsdp")
    where = jnp.stack([r & 1, (r >> 1) & 3, r >> 3, f & 3, f >> 2]).astype(jnp.int32)
    return both_steps(where, pseudo_grad, anchor, momentum, hidden, grad_out)


def solution(mesh):
    placed = (
        P("replica", "fsdp", None),
        P("fsdp", "replica"),
        P("fsdp", "replica"),
        P("replica", "fsdp", None),
        P("replica", "fsdp", None),
    )
    return jax.shard_map(
        on_device,
        mesh=mesh,
        in_specs=placed,
        out_specs=(
            P("fsdp", "replica"),
            P("fsdp", "replica"),
            P("fsdp", None),
            P("replica", "fsdp", None),
        ),
        check_vma=False,
    )
```

```python
import functools

import jax
import jax.numpy as jnp
from jax import lax
from jax.experimental import pallas as pl
from jax.experimental.pallas import tpu as pltpu
from jax.sharding import PartitionSpec as P

BLOCK = 128
EPSILON = 1e-06
TOP_EXPONENT = 6
OUTER_MOMENTUM = 0.9
OUTER_RATE = 0.7
TURNS = (1, 3, 2)
LIMIT = 16 * 1024 * 1024

ANY = pl.BlockSpec(memory_space=pl.ANY)
VMEM = pl.BlockSpec(memory_space=pltpu.VMEM)
HBM = pl.BlockSpec(memory_space=pltpu.HBM)
SMEM = pl.BlockSpec(memory_space=pltpu.SMEM)


def replica_perm(move):
    pairs = []
    for z in range(4):
        for x in range(4):
            for c in range(2):
                to = move(z, x, c)
                pairs.append((z * 8 + x * 2 + c, to[0] * 8 + to[1] * 2 + to[2]))
    return pairs


def fsdp_perm(move):
    pairs = []
    for h in range(2):
        for y in range(4):
            to = move(h, y)
            pairs.append((h * 4 + y, to[0] * 4 + to[1]))
    return pairs


def to_core(a):
    return lax.ppermute(a, "replica", replica_perm(lambda z, x, c: (z, x, 1 - c)))


def to_x(a, k):
    return lax.ppermute(a, "replica", replica_perm(lambda z, x, c: (z, (x + k) % 4, c)))


def to_z(a, k):
    return lax.ppermute(a, "replica", replica_perm(lambda z, x, c: (z ^ k, x, c)))


def to_y(a, k):
    return lax.ppermute(a, "fsdp", fsdp_perm(lambda h, y: (h, (y + k) % 4)))


def to_half(a):
    return lax.ppermute(a, "fsdp", fsdp_perm(lambda h, y: (1 - h, y)))


def call(kernel, out, ins, specs, out_specs=None, scratch=(), cost=0, alias=None):
    return pl.pallas_call(
        kernel,
        out_shape=out,
        in_specs=specs,
        out_specs=out_specs if out_specs is not None else [VMEM] * len(out),
        scratch_shapes=list(scratch),
        input_output_aliases=alias or {},
        cost_estimate=pl.CostEstimate(flops=cost, bytes_accessed=cost, transcendentals=0),
        compiler_params=pltpu.CompilerParams(vmem_limit_bytes=LIMIT),
    )(*ins)


def gate_kernel(*refs):
    pass


def gate(after, *arrays):
    n = len(arrays)
    return call(
        gate_kernel,
        [jax.ShapeDtypeStruct(a.shape, a.dtype) for a in arrays],
        (*arrays, *after),
        [ANY] * (n + len(after)),
        [ANY] * n,
        cost=1 << 10,
        alias={i: i for i in range(n)},
    )


def bf16(*shape):
    return jax.ShapeDtypeStruct(shape, jnp.bfloat16)


def f32(*shape):
    return jax.ShapeDtypeStruct(shape, jnp.float32)


def split_kernel(where, grad, keep, give, keep_peak, give_peak, rows, tops, sems):
    core = where[0]

    def fetch(i):
        part = pl.ds(pl.multiple_of(i * 32, 32), 32)
        return pltpu.make_async_copy(grad.at[0, part, :], rows.at[part, :], sems.at[i])

    for i in range(4):
        fetch(i).start()
    lanes = lax.broadcasted_iota(jnp.int32, (32, 128), 1)

    def chunk(i, carry):
        fetch(i).wait()
        part = pl.ds(pl.multiple_of(i * 32, 32), 32)
        acc = jnp.zeros((32, 128), jnp.float32)
        for n in range(16):
            for k, (side, out) in enumerate(((core, keep), (1 - core, give))):
                start = pl.multiple_of(n * 512 + side * 256, 256)
                value = rows[part, pl.ds(start, 256)]
                out[n, part, :] = value
                size = jnp.abs(value)
                for b in range(2):
                    block = size[:, b * BLOCK : (b + 1) * BLOCK].astype(jnp.float32)
                    top = jnp.max(block, axis=1, keepdims=True)
                    acc = jnp.where(lanes == 32 * k + 2 * n + b, top, acc)
        tops[part, :] = acc
        return carry

    lax.fori_loop(0, 4, chunk, 0)
    flat = tops[...].T
    keep_peak[...] = flat[:32].astype(jnp.bfloat16)
    give_peak[...] = flat[32:64].astype(jnp.bfloat16)


def top_kernel(a0, a1, a2, a3, *rest):
    out = rest[-1]
    out[...] = jnp.maximum(jnp.maximum(a0[...], a1[...]), jnp.maximum(a2[...], a3[...]))


def scale_of(peak):
    bounded = peak + EPSILON
    scale = jnp.ones_like(bounded)
    for e in range(1, 26):
        scale = jnp.where(bounded <= 2.0 ** (TOP_EXPONENT - e), 2.0**e, scale)
    return scale


def encode_kernel(where, mine, other, p0, p1, p2, p3, after, o0, o1, o2, o3, step, scales):
    x, z = where[1], where[2]
    peak = jnp.maximum(
        jnp.maximum(p0[...].astype(jnp.float32), p1[...].astype(jnp.float32)),
        jnp.maximum(p2[...].astype(jnp.float32), p3[...].astype(jnp.float32)),
    )
    scale = scale_of(peak)
    wide = jnp.concatenate([scale, jnp.ones((96, 128), jnp.float32)], axis=0).T
    for n in range(32):
        scales[n // 2, :, (n % 2) * BLOCK : (n % 2 + 1) * BLOCK] = jnp.broadcast_to(
            wide[:, n : n + 1], (128, 128)
        )
    step[...] = 1.0 / (scales[z * 4 + x] * 32.0)
    for k, out in enumerate((o0, o1, o2, o3)):
        column = lax.rem(x + k, 4)
        for level in range(4):
            n = level * 4 + column
            s = scales[n]
            first = jnp.floor(mine[n].astype(jnp.float32) * s + 0.5)
            second = jnp.floor(other[n].astype(jnp.float32) * s + 0.5)
            out[level] = (first + second).astype(jnp.bfloat16)


def sum_x_kernel(where, a0, a1, a2, a3, o0, o1, o2, o3):
    z = where[2]
    for k, out in enumerate((o0, o1, o2, o3)):
        level = z ^ k
        parts = [a[level].astype(jnp.float32) for a in (a0, a1, a2, a3)]
        out[...] = (((parts[0] + parts[1]) + (parts[2] + parts[3]))).astype(out.dtype)


def update_kernel(a0, a1, a2, a3, step, anchor, momentum, after1, after2, anchor_out, momentum_out, params):
    parts = [a[...].astype(jnp.float32) for a in (a0, a1, a2, a3)]
    total = (parts[0] + parts[1]) + (parts[2] + parts[3])
    delta = total * step[...]
    fresh = OUTER_MOMENTUM * momentum[...] + delta
    moved = anchor[...] - OUTER_RATE * (delta + OUTER_MOMENTUM * fresh)
    momentum_out[...] = fresh
    anchor_out[...] = moved
    params[...] = moved.astype(jnp.bfloat16)


def gather_z_kernel(where, a0, a1, a2, a3, after, out):
    z = where[2]
    for k, a in enumerate((a0, a1, a2, a3)):
        out[z ^ k] = a[...]


def place_copies(sides, turns, where, blocks, out, sems):
    core, x = where[0], where[1]
    copies = []
    for block, side, turn in zip(blocks, sides, turns):
        column = lax.rem(x + 4 - turn, 4)
        half = core if side == 0 else 1 - core
        for level in range(4):
            start = pl.multiple_of((level * 4 + column) * 512 + half * 256, 256)
            copies.append(
                pltpu.make_async_copy(
                    block.at[level], out.at[:, pl.ds(start, 256)], sems.at[len(copies)]
                )
            )
    return copies


def place_kernel(sides, turns, where, *refs):
    copies = place_copies(sides, turns, where, refs[: len(sides)], refs[-2], refs[-1])
    for copy in copies:
        copy.start()
    for copy in copies:
        copy.wait()


def add_halves_kernel(keep, came, out, token):
    out[0] = (keep[...] + came[...].astype(jnp.float32)).astype(jnp.bfloat16)
    token[...] = jnp.zeros_like(token)


def place(where, out, items):
    blocks, sides, turns = zip(*items)
    given = [] if out is None else [out]
    return call(
        functools.partial(place_kernel, sides, turns),
        [bf16(128, 8192)],
        (where, *blocks, *given),
        [SMEM] + [VMEM] * len(blocks) + [HBM] * len(given),
        [HBM],
        scratch=[pltpu.SemaphoreType.DMA((4 * len(blocks),))],
        cost=1 << 18,
        alias={1 + len(blocks): 0} if given else None,
    )[0]


def both_steps(where, pseudo_grad, anchor, momentum, hidden, grad_out):
    mine, give, peak, other_peak = call(
        split_kernel,
        [bf16(16, 128, 256)] * 2 + [bf16(32, 128)] * 2,
        (where, pltpu.with_memory_space_constraint(pseudo_grad, pltpu.HBM)),
        [SMEM, HBM],
        scratch=[
            pltpu.VMEM((128, 8192), jnp.bfloat16),
            pltpu.VMEM((128, 128), jnp.float32),
            pltpu.SemaphoreType.DMA((4,)),
        ],
        cost=1 << 21,
    )
    peak = jnp.maximum(peak, to_core(other_peak))
    (give,) = gate((peak,), give)
    other = to_core(give)
    near = [to_x(peak, k) for k in (1, 3, 2)]
    pieces = inner_pieces(where, hidden, grad_out, peak, 0)
    (peak,) = call(
        top_kernel,
        [bf16(32, 128)],
        (peak, *near, other, pieces[0]),
        [VMEM] * 4 + [ANY] * 2,
        cost=1 << 16,
    )
    peaks = [peak] + [to_z(peak, k) for k in (1, 2, 3)]
    pieces = list(inner_pieces(where, hidden, grad_out, peak, 1, pieces))
    *codes, step = call(
        encode_kernel,
        [bf16(4, 128, 256)] * 4 + [f32(128, 256)],
        (where, mine, other, *peaks, pieces[0]),
        [SMEM] + [VMEM] * 6 + [ANY],
        scratch=[pltpu.VMEM((16, 128, 256), jnp.float32)],
        cost=1 << 22,
    )
    parts = [codes[0]] + [to_x(codes[k], k) for k in (2, 1, 3)]
    pieces[1], pieces[3] = gate((codes[0],), pieces[1], pieces[3])
    pieces[1], pieces[3] = to_y(pieces[1], 1), to_y(pieces[3], 3)
    first_part = parts[2]
    sums = list(
        call(
            sum_x_kernel,
            [f32(128, 256)] + [bf16(128, 256)] * 3,
            (where, *parts),
            [SMEM] + [VMEM] * 4,
            cost=1 << 32,
        )
    )
    (pieces[2],) = gate((first_part,), pieces[2])
    inner_keep, inner_give = call(
        sum_y_kernel,
        [f32(16, 8192), bf16(16, 8192)],
        (where, pieces[0], pieces[1], to_y(pieces[2], 2), pieces[3]),
        [SMEM] + [VMEM] * 4,
        cost=1 << 21,
    )
    (sums[1],) = gate((pieces[1],), sums[1])
    parts = [sums[0]] + [to_z(sums[k], k) for k in (3, 2, 1)]
    anchor_next, momentum_next, params = call(
        update_kernel,
        [f32(128, 256), f32(128, 256), bf16(128, 256)],
        (*parts, step, anchor, momentum, pieces[1], pieces[3]),
        [VMEM] * 7 + [ANY] * 2,
        cost=1 << 19,
    )
    parts = [params] + [to_z(params, k) for k in (1, 2, 3)]
    (block,) = call(
        gather_z_kernel,
        [bf16(4, 128, 256)],
        (where, *parts, inner_give),
        [SMEM] + [VMEM] * 4 + [ANY],
    )
    far = [to_x(block, k) for k in TURNS]
    twin = to_core(block)
    grad_shard, token = call(
        add_halves_kernel,
        [bf16(1, 16, 8192), f32(8, 128)],
        (inner_keep, to_half(inner_give)),
        [VMEM] * 2,
        cost=1 << 20,
    )
    far = gate((token,), *far)
    twins = [to_core(a) for a in far]
    params_next = place(
        where, None, [(a, 0, k) for k, a in zip((0, *TURNS), (block, *far))] + [(twin, 1, 0)]
    )
    params_next = place(where, params_next, [(a, 1, k) for k, a in zip(TURNS, twins)])
    return anchor_next, momentum_next, params_next, grad_shard


def product_kernel(where, hidden, grad, after, *refs):
    o0, o1, o2, o3, left, whole = refs[-6:]

    @pl.when(pl.program_id(0) == 0)
    def _():
        left[...] = hidden[0].astype(jnp.float32).T.astype(jnp.bfloat16)

    whole[...] = jnp.dot(
        left[...], grad[0], preferred_element_type=jnp.float32
    ).astype(jnp.bfloat16)
    y = where[3]
    for k, out in enumerate((o0, o1, o2, o3)):
        for half in range(2):
            start = pl.multiple_of(half * 64 + lax.rem(y + k, 4) * 16, 16)
            out[half * 16 : half * 16 + 16, :] = whole[pl.ds(start, 16), :]


def sum_y_kernel(where, a0, a1, a2, a3, keep, give):
    half = where[4]
    for side, out in ((half, keep), (1 - half, give)):
        rows = pl.ds(pl.multiple_of(side * 16, 16), 16)
        parts = [a[rows, :].astype(jnp.float32) for a in (a0, a1, a2, a3)]
        out[...] = ((parts[0] + parts[1]) + (parts[2] + parts[3])).astype(out.dtype)


def inner_pieces(where, hidden, grad_out, after, part, given=()):
    tile = 2048
    steps = 8192 // tile // 2
    return pl.pallas_call(
        product_kernel,
        grid=(steps,),
        out_shape=[bf16(32, 8192)] * 4,
        in_specs=[
            SMEM,
            pl.BlockSpec((1, 384, 128), lambda i: (0, 0, 0)),
            pl.BlockSpec((1, 384, tile), lambda i: (0, 0, i + part * steps)),
            ANY,
        ]
        + [ANY] * len(given),
        out_specs=[pl.BlockSpec((32, tile), lambda i: (0, i + part * steps))] * 4,
        scratch_shapes=[
            pltpu.VMEM((128, 384), jnp.bfloat16),
            pltpu.VMEM((128, tile), jnp.bfloat16),
        ],
        input_output_aliases={4 + k: k for k in range(len(given))},
        cost_estimate=pl.CostEstimate(
            flops=128 * 384 * 8192, bytes_accessed=1 << 22, transcendentals=0
        ),
        compiler_params=pltpu.CompilerParams(vmem_limit_bytes=LIMIT),
    )(where, hidden, pltpu.with_memory_space_constraint(grad_out, pltpu.HBM), after, *given)


def on_device(pseudo_grad, anchor, momentum, hidden, grad_out):
    r, f = lax.axis_index("replica"), lax.axis_index("fsdp")
    where = jnp.stack([r & 1, (r >> 1) & 3, r >> 3, f & 3, f >> 2]).astype(jnp.int32)
    return both_steps(where, pseudo_grad, anchor, momentum, hidden, grad_out)


def solution(mesh):
    placed = (
        P("replica", "fsdp", None),
        P("fsdp", "replica"),
        P("fsdp", "replica"),
        P("replica", "fsdp", None),
        P("replica", "fsdp", None),
    )
    return jax.shard_map(
        on_device,
        mesh=mesh,
        in_specs=placed,
        out_specs=(
            P("fsdp", "replica"),
            P("fsdp", "replica"),
            P("fsdp", None),
            P("replica", "fsdp", None),
        ),
        check_vma=False,
    )
```

```python
import functools

import jax
import jax.numpy as jnp
from jax import lax
from jax.experimental import pallas as pl
from jax.experimental.pallas import tpu as pltpu
from jax.sharding import PartitionSpec as P

BLOCK = 128
EPSILON = 1e-06
TOP_EXPONENT = 6
OUTER_MOMENTUM = 0.9
OUTER_RATE = 0.7
LIMIT = 16 * 1024 * 1024

ANY = pl.BlockSpec(memory_space=pl.ANY)
VMEM = pl.BlockSpec(memory_space=pltpu.VMEM)
HBM = pl.BlockSpec(memory_space=pltpu.HBM)
SMEM = pl.BlockSpec(memory_space=pltpu.SMEM)


def replica_perm(move):
    pairs = []
    for z in range(4):
        for x in range(4):
            for c in range(2):
                to = move(z, x, c)
                pairs.append((z * 8 + x * 2 + c, to[0] * 8 + to[1] * 2 + to[2]))
    return pairs


def fsdp_perm(move):
    pairs = []
    for h in range(2):
        for y in range(4):
            to = move(h, y)
            pairs.append((h * 4 + y, to[0] * 4 + to[1]))
    return pairs


def to_core(a):
    return lax.ppermute(a, "replica", replica_perm(lambda z, x, c: (z, x, 1 - c)))


def to_x(a, k):
    return lax.ppermute(a, "replica", replica_perm(lambda z, x, c: (z, (x + k) % 4, c)))


def to_z(a, k):
    return lax.ppermute(a, "replica", replica_perm(lambda z, x, c: (z ^ k, x, c)))


def to_y(a, k):
    return lax.ppermute(a, "fsdp", fsdp_perm(lambda h, y: (h, (y + k) % 4)))


def to_half(a):
    return lax.ppermute(a, "fsdp", fsdp_perm(lambda h, y: (1 - h, y)))


def call(kernel, out, ins, specs, out_specs=None, scratch=(), cost=0, alias=None):
    return pl.pallas_call(
        kernel,
        out_shape=out,
        in_specs=specs,
        out_specs=out_specs if out_specs is not None else [VMEM] * len(out),
        scratch_shapes=list(scratch),
        input_output_aliases=alias or {},
        cost_estimate=pl.CostEstimate(flops=cost, bytes_accessed=cost, transcendentals=0),
        compiler_params=pltpu.CompilerParams(vmem_limit_bytes=LIMIT),
    )(*ins)


def gate_kernel(*refs):
    pass


def gate(after, *arrays):
    n = len(arrays)
    return call(
        gate_kernel,
        [jax.ShapeDtypeStruct(a.shape, a.dtype) for a in arrays],
        (*arrays, *after),
        [ANY] * (n + len(after)),
        [ANY] * n,
        cost=1 << 10,
        alias={i: i for i in range(n)},
    )


def bf16(*shape):
    return jax.ShapeDtypeStruct(shape, jnp.bfloat16)


def f32(*shape):
    return jax.ShapeDtypeStruct(shape, jnp.float32)


def split_kernel(where, grad, keep, give, keep_peak, give_peak, rows, tops, sems):
    core = where[0]

    def fetch(i):
        part = pl.ds(pl.multiple_of(i * 32, 32), 32)
        return pltpu.make_async_copy(grad.at[0, part, :], rows.at[part, :], sems.at[i])

    for i in range(4):
        fetch(i).start()
    lanes = lax.broadcasted_iota(jnp.int32, (32, 128), 1)

    def chunk(i, carry):
        fetch(i).wait()
        part = pl.ds(pl.multiple_of(i * 32, 32), 32)
        acc = jnp.zeros((32, 128), jnp.float32)
        for n in range(16):
            for k, (side, out) in enumerate(((core, keep), (1 - core, give))):
                start = pl.multiple_of(n * 512 + side * 256, 256)
                value = rows[part, pl.ds(start, 256)]
                out[n, part, :] = value
                size = jnp.abs(value)
                for b in range(2):
                    block = size[:, b * BLOCK : (b + 1) * BLOCK].astype(jnp.float32)
                    top = jnp.max(block, axis=1, keepdims=True)
                    acc = jnp.where(lanes == 32 * k + 2 * n + b, top, acc)
        tops[part, :] = acc
        return carry

    lax.fori_loop(0, 4, chunk, 0)
    flat = tops[...].T
    keep_peak[...] = flat[:32].astype(jnp.bfloat16)
    give_peak[...] = flat[32:64].astype(jnp.bfloat16)


def top_kernel(a0, a1, a2, a3, *rest):
    out = rest[-1]
    out[...] = jnp.maximum(jnp.maximum(a0[...], a1[...]), jnp.maximum(a2[...], a3[...]))


def scale_of(peak):
    bounded = peak + EPSILON
    scale = jnp.ones_like(bounded)
    for e in range(1, 26):
        scale = jnp.where(bounded <= 2.0 ** (TOP_EXPONENT - e), 2.0**e, scale)
    return scale


def encode_kernel(where, mine, other, p0, p1, p2, p3, after, o0, o1, o2, o3, step, scales):
    x, z = where[1], where[2]
    peak = jnp.maximum(
        jnp.maximum(p0[...].astype(jnp.float32), p1[...].astype(jnp.float32)),
        jnp.maximum(p2[...].astype(jnp.float32), p3[...].astype(jnp.float32)),
    )
    scale = scale_of(peak)
    wide = jnp.concatenate([scale, jnp.ones((96, 128), jnp.float32)], axis=0).T
    for n in range(32):
        scales[n // 2, :, (n % 2) * BLOCK : (n % 2 + 1) * BLOCK] = jnp.broadcast_to(
            wide[:, n : n + 1], (128, 128)
        )
    step[...] = 1.0 / (scales[z * 4 + x] * 32.0)
    for k, out in enumerate((o0, o1, o2, o3)):
        column = lax.rem(x + k, 4)
        for level in range(4):
            n = level * 4 + column
            s = scales[n]
            first = jnp.floor(mine[n].astype(jnp.float32) * s + 0.5)
            second = jnp.floor(other[n].astype(jnp.float32) * s + 0.5)
            out[level] = (first + second).astype(jnp.bfloat16)


def sum_x_kernel(where, a0, a1, a2, a3, o0, o1, o2, o3):
    z = where[2]
    for k, out in enumerate((o0, o1, o2, o3)):
        level = z ^ k
        parts = [a[level].astype(jnp.float32) for a in (a0, a1, a2, a3)]
        out[...] = (((parts[0] + parts[1]) + (parts[2] + parts[3]))).astype(out.dtype)


def update_kernel(a0, a1, a2, a3, step, anchor, momentum, after1, after2, anchor_out, momentum_out, params):
    parts = [a[...].astype(jnp.float32) for a in (a0, a1, a2, a3)]
    total = (parts[0] + parts[1]) + (parts[2] + parts[3])
    delta = total * step[...]
    fresh = OUTER_MOMENTUM * momentum[...] + delta
    moved = anchor[...] - OUTER_RATE * (delta + OUTER_MOMENTUM * fresh)
    momentum_out[...] = fresh
    anchor_out[...] = moved
    params[...] = moved.astype(jnp.bfloat16)


def gather_z_kernel(where, a0, a1, a2, a3, out):
    z = where[2]
    for k, a in enumerate((a0, a1, a2, a3)):
        out[z ^ k] = a[...]


def place_copies(sides, turns, where, blocks, out, sems):
    core, x = where[0], where[1]
    copies = []
    for block, side, turn in zip(blocks, sides, turns):
        column = lax.rem(x + 4 - turn, 4)
        half = core if side == 0 else 1 - core
        for level in range(4):
            start = pl.multiple_of((level * 4 + column) * 512 + half * 256, 256)
            copies.append(
                pltpu.make_async_copy(
                    block.at[level], out.at[:, pl.ds(start, 256)], sems.at[len(copies)]
                )
            )
    return copies


def place_kernel(sides, turns, where, *refs):
    copies = place_copies(sides, turns, where, refs[: len(sides)], refs[-2], refs[-1])
    for copy in copies:
        copy.start()
    for copy in copies:
        copy.wait()


def add_halves_kernel(keep, came, out):
    out[0] = (keep[...] + came[...].astype(jnp.float32)).astype(jnp.bfloat16)


def place(where, out, items):
    blocks, sides, turns = zip(*items)
    given = [] if out is None else [out]
    return call(
        functools.partial(place_kernel, sides, turns),
        [bf16(128, 8192)],
        (where, *blocks, *given),
        [SMEM] + [VMEM] * len(blocks) + [HBM] * len(given),
        [HBM],
        scratch=[pltpu.SemaphoreType.DMA((4 * len(blocks),))],
        cost=1 << 18,
        alias={1 + len(blocks): 0} if given else None,
    )[0]


def both_steps(where, pseudo_grad, anchor, momentum, hidden, grad_out):
    mine, give, peak, other_peak = call(
        split_kernel,
        [bf16(16, 128, 256)] * 2 + [bf16(32, 128)] * 2,
        (where, pltpu.with_memory_space_constraint(pseudo_grad, pltpu.HBM)),
        [SMEM, HBM],
        scratch=[
            pltpu.VMEM((128, 8192), jnp.bfloat16),
            pltpu.VMEM((128, 128), jnp.float32),
            pltpu.SemaphoreType.DMA((4,)),
        ],
        cost=1 << 21,
    )
    peak = jnp.maximum(peak, to_core(other_peak))
    (give,) = gate((peak,), give)
    other = to_core(give)
    near = [to_x(peak, k) for k in (1, 2, 3)]
    pieces = inner_pieces(where, hidden, grad_out, peak, 0)
    (peak,) = call(
        top_kernel,
        [bf16(32, 128)],
        (peak, *near, other, pieces[0]),
        [VMEM] * 4 + [ANY] * 2,
        cost=1 << 16,
    )
    peaks = [peak] + [to_z(peak, k) for k in (1, 2, 3)]
    pieces = list(inner_pieces(where, hidden, grad_out, peak, 1, pieces))
    *codes, step = call(
        encode_kernel,
        [bf16(4, 128, 256)] * 4 + [f32(128, 256)],
        (where, mine, other, *peaks, pieces[0]),
        [SMEM] + [VMEM] * 6 + [ANY],
        scratch=[pltpu.VMEM((16, 128, 256), jnp.float32)],
        cost=1 << 22,
    )
    parts = [codes[0]] + [to_x(codes[k], k) for k in (1, 2, 3)]
    pieces[1], pieces[3] = gate((codes[0],), pieces[1], pieces[3])
    pieces[1], pieces[3] = to_y(pieces[1], 1), to_y(pieces[3], 3)
    sums = call(
        sum_x_kernel,
        [f32(128, 256)] + [bf16(128, 256)] * 3,
        (where, *parts),
        [SMEM] + [VMEM] * 4,
        cost=1 << 31,
    )
    (pieces[2],) = gate((sums[0],), pieces[2])
    inner_keep, inner_give = call(
        sum_y_kernel,
        [f32(16, 8192), bf16(16, 8192)],
        (where, pieces[0], pieces[1], to_y(pieces[2], 2), pieces[3]),
        [SMEM] + [VMEM] * 4,
        cost=1 << 21,
    )
    parts = [sums[0]] + [to_z(sums[k], k) for k in (1, 2, 3)]
    anchor_next, momentum_next, params = call(
        update_kernel,
        [f32(128, 256), f32(128, 256), bf16(128, 256)],
        (*parts, step, anchor, momentum, pieces[1], pieces[3]),
        [VMEM] * 7 + [ANY] * 2,
        cost=1 << 32,
    )
    parts = [params] + [to_z(params, k) for k in (1, 2, 3)]
    (block,) = call(
        gather_z_kernel,
        [bf16(4, 128, 256)],
        (where, *parts),
        [SMEM] + [VMEM] * 4,
    )
    far = [to_x(block, k) for k in (1, 2, 3)]
    twin = to_core(block)
    (grad_shard,) = call(
        add_halves_kernel,
        [bf16(1, 16, 8192)],
        (inner_keep, to_half(inner_give)),
        [VMEM] * 2,
        cost=1 << 20,
    )
    twins = [to_core(a) for a in far]
    params_next = place(where, None, [(block, 0, 0), (twin, 1, 0)])
    params_next = place(where, params_next, [(a, 0, k) for k, a in zip((1, 2, 3), far)])
    params_next = place(where, params_next, [(a, 1, k) for k, a in zip((1, 2, 3), twins)])
    return anchor_next, momentum_next, params_next, grad_shard


def product_kernel(where, hidden, grad, after, *refs):
    o0, o1, o2, o3, left, whole = refs[-6:]

    @pl.when(pl.program_id(0) == 0)
    def _():
        left[...] = hidden[0].astype(jnp.float32).T.astype(jnp.bfloat16)

    whole[...] = jnp.dot(
        left[...], grad[0], preferred_element_type=jnp.float32
    ).astype(jnp.bfloat16)
    y = where[3]
    for k, out in enumerate((o0, o1, o2, o3)):
        for half in range(2):
            start = pl.multiple_of(half * 64 + lax.rem(y + k, 4) * 16, 16)
            out[half * 16 : half * 16 + 16, :] = whole[pl.ds(start, 16), :]


def sum_y_kernel(where, a0, a1, a2, a3, keep, give):
    half = where[4]
    for side, out in ((half, keep), (1 - half, give)):
        rows = pl.ds(pl.multiple_of(side * 16, 16), 16)
        parts = [a[rows, :].astype(jnp.float32) for a in (a0, a1, a2, a3)]
        out[...] = ((parts[0] + parts[1]) + (parts[2] + parts[3])).astype(out.dtype)


def inner_pieces(where, hidden, grad_out, after, part, given=()):
    tile = 2048
    steps = 8192 // tile // 2
    return pl.pallas_call(
        product_kernel,
        grid=(steps,),
        out_shape=[bf16(32, 8192)] * 4,
        in_specs=[
            SMEM,
            pl.BlockSpec((1, 384, 128), lambda i: (0, 0, 0)),
            pl.BlockSpec((1, 384, tile), lambda i: (0, 0, i + part * steps)),
            ANY,
        ]
        + [ANY] * len(given),
        out_specs=[pl.BlockSpec((32, tile), lambda i: (0, i + part * steps))] * 4,
        scratch_shapes=[
            pltpu.VMEM((128, 384), jnp.bfloat16),
            pltpu.VMEM((128, tile), jnp.bfloat16),
        ],
        input_output_aliases={4 + k: k for k in range(len(given))},
        cost_estimate=pl.CostEstimate(
            flops=128 * 384 * 8192, bytes_accessed=1 << 22, transcendentals=0
        ),
        compiler_params=pltpu.CompilerParams(vmem_limit_bytes=LIMIT),
    )(where, hidden, pltpu.with_memory_space_constraint(grad_out, pltpu.HBM), after, *given)


def on_device(pseudo_grad, anchor, momentum, hidden, grad_out):
    r, f = lax.axis_index("replica"), lax.axis_index("fsdp")
    where = jnp.stack([r & 1, (r >> 1) & 3, r >> 3, f & 3, f >> 2]).astype(jnp.int32)
    return both_steps(where, pseudo_grad, anchor, momentum, hidden, grad_out)


def solution(mesh):
    placed = (
        P("replica", "fsdp", None),
        P("fsdp", "replica"),
        P("fsdp", "replica"),
        P("replica", "fsdp", None),
        P("replica", "fsdp", None),
    )
    return jax.shard_map(
        on_device,
        mesh=mesh,
        in_specs=placed,
        out_specs=(
            P("fsdp", "replica"),
            P("fsdp", "replica"),
            P("fsdp", None),
            P("replica", "fsdp", None),
        ),
        check_vma=False,
    )
```

```python
import functools

import jax
import jax.numpy as jnp
from jax import lax
from jax.experimental import pallas as pl
from jax.experimental.pallas import tpu as pltpu
from jax.sharding import PartitionSpec as P

BLOCK = 128
EPSILON = 1e-06
TOP_EXPONENT = 6
OUTER_MOMENTUM = 0.9
OUTER_RATE = 0.7
LIMIT = 16 * 1024 * 1024

ANY = pl.BlockSpec(memory_space=pl.ANY)
VMEM = pl.BlockSpec(memory_space=pltpu.VMEM)
HBM = pl.BlockSpec(memory_space=pltpu.HBM)
SMEM = pl.BlockSpec(memory_space=pltpu.SMEM)


def replica_perm(move):
    pairs = []
    for z in range(4):
        for x in range(4):
            for c in range(2):
                to = move(z, x, c)
                pairs.append((z * 8 + x * 2 + c, to[0] * 8 + to[1] * 2 + to[2]))
    return pairs


def fsdp_perm(move):
    pairs = []
    for h in range(2):
        for y in range(4):
            to = move(h, y)
            pairs.append((h * 4 + y, to[0] * 4 + to[1]))
    return pairs


def to_core(a):
    return lax.ppermute(a, "replica", replica_perm(lambda z, x, c: (z, x, 1 - c)))


def to_x(a, k):
    return lax.ppermute(a, "replica", replica_perm(lambda z, x, c: (z, (x + k) % 4, c)))


def to_z(a, k):
    return lax.ppermute(a, "replica", replica_perm(lambda z, x, c: (z ^ k, x, c)))


def to_y(a, k):
    return lax.ppermute(a, "fsdp", fsdp_perm(lambda h, y: (h, (y + k) % 4)))


def to_half(a):
    return lax.ppermute(a, "fsdp", fsdp_perm(lambda h, y: (1 - h, y)))


def call(kernel, out, ins, specs, out_specs=None, scratch=(), cost=0, alias=None):
    return pl.pallas_call(
        kernel,
        out_shape=out,
        in_specs=specs,
        out_specs=out_specs if out_specs is not None else [VMEM] * len(out),
        scratch_shapes=list(scratch),
        input_output_aliases=alias or {},
        cost_estimate=pl.CostEstimate(flops=cost, bytes_accessed=cost, transcendentals=0),
        compiler_params=pltpu.CompilerParams(vmem_limit_bytes=LIMIT),
    )(*ins)


def gate_kernel(*refs):
    pass


def gate(after, *arrays):
    n = len(arrays)
    return call(
        gate_kernel,
        [jax.ShapeDtypeStruct(a.shape, a.dtype) for a in arrays],
        (*arrays, *after),
        [ANY] * (n + len(after)),
        [ANY] * n,
        cost=1 << 10,
        alias={i: i for i in range(n)},
    )


def bf16(*shape):
    return jax.ShapeDtypeStruct(shape, jnp.bfloat16)


def f32(*shape):
    return jax.ShapeDtypeStruct(shape, jnp.float32)


def split_kernel(where, grad, keep, give, keep_peak, give_peak, rows, tops, sems):
    core = where[0]

    def fetch(i):
        part = pl.ds(pl.multiple_of(i * 32, 32), 32)
        return pltpu.make_async_copy(grad.at[0, part, :], rows.at[part, :], sems.at[i])

    for i in range(4):
        fetch(i).start()
    lanes = lax.broadcasted_iota(jnp.int32, (32, 128), 1)

    def chunk(i, carry):
        fetch(i).wait()
        part = pl.ds(pl.multiple_of(i * 32, 32), 32)
        acc = jnp.zeros((32, 128), jnp.float32)
        for n in range(16):
            for k, (side, out) in enumerate(((core, keep), (1 - core, give))):
                start = pl.multiple_of(n * 512 + side * 256, 256)
                value = rows[part, pl.ds(start, 256)]
                out[n, part, :] = value
                size = jnp.abs(value)
                for b in range(2):
                    block = size[:, b * BLOCK : (b + 1) * BLOCK].astype(jnp.float32)
                    top = jnp.max(block, axis=1, keepdims=True)
                    acc = jnp.where(lanes == 32 * k + 2 * n + b, top, acc)
        tops[part, :] = acc
        return carry

    lax.fori_loop(0, 4, chunk, 0)
    flat = tops[...].T
    keep_peak[...] = flat[:32].astype(jnp.bfloat16)
    give_peak[...] = flat[32:64].astype(jnp.bfloat16)


def top_kernel(a0, a1, a2, a3, *rest):
    out = rest[-1]
    out[...] = jnp.maximum(jnp.maximum(a0[...], a1[...]), jnp.maximum(a2[...], a3[...]))


def scale_of(peak):
    bounded = peak + EPSILON
    scale = jnp.ones_like(bounded)
    for e in range(1, 26):
        scale = jnp.where(bounded <= 2.0 ** (TOP_EXPONENT - e), 2.0**e, scale)
    return scale


def encode_kernel(where, mine, other, p0, p1, p2, p3, after, o0, o1, o2, o3, step, scales):
    x, z = where[1], where[2]
    peak = jnp.maximum(
        jnp.maximum(p0[...].astype(jnp.float32), p1[...].astype(jnp.float32)),
        jnp.maximum(p2[...].astype(jnp.float32), p3[...].astype(jnp.float32)),
    )
    scale = scale_of(peak)
    wide = jnp.concatenate([scale, jnp.ones((96, 128), jnp.float32)], axis=0).T
    for n in range(32):
        scales[n // 2, :, (n % 2) * BLOCK : (n % 2 + 1) * BLOCK] = jnp.broadcast_to(
            wide[:, n : n + 1], (128, 128)
        )
    step[...] = 1.0 / (scales[z * 4 + x] * 32.0)
    for k, out in enumerate((o0, o1, o2, o3)):
        column = lax.rem(x + k, 4)
        for level in range(4):
            n = level * 4 + column
            s = scales[n]
            first = jnp.floor(mine[n].astype(jnp.float32) * s + 0.5)
            second = jnp.floor(other[n].astype(jnp.float32) * s + 0.5)
            out[level] = (first + second).astype(jnp.bfloat16)


def sum_x_kernel(where, a0, a1, a2, a3, o0, o1, o2, o3):
    z = where[2]
    for k, out in enumerate((o0, o1, o2, o3)):
        level = z ^ k
        parts = [a[level].astype(jnp.float32) for a in (a0, a1, a2, a3)]
        out[...] = (((parts[0] + parts[1]) + (parts[2] + parts[3]))).astype(out.dtype)


def update_kernel(a0, a1, a2, a3, step, anchor, momentum, after1, after2, anchor_out, momentum_out, params):
    parts = [a[...].astype(jnp.float32) for a in (a0, a1, a2, a3)]
    total = (parts[0] + parts[1]) + (parts[2] + parts[3])
    delta = total * step[...]
    fresh = OUTER_MOMENTUM * momentum[...] + delta
    moved = anchor[...] - OUTER_RATE * (delta + OUTER_MOMENTUM * fresh)
    momentum_out[...] = fresh
    anchor_out[...] = moved
    params[...] = moved.astype(jnp.bfloat16)


def gather_z_kernel(where, a0, a1, a2, a3, after, out):
    z = where[2]
    for k, a in enumerate((a0, a1, a2, a3)):
        out[z ^ k] = a[...]


def place_copies(sides, turns, where, blocks, out, sems):
    core, x = where[0], where[1]
    copies = []
    for block, side, turn in zip(blocks, sides, turns):
        column = lax.rem(x + 4 - turn, 4)
        half = core if side == 0 else 1 - core
        for level in range(4):
            start = pl.multiple_of((level * 4 + column) * 512 + half * 256, 256)
            copies.append(
                pltpu.make_async_copy(
                    block.at[level], out.at[:, pl.ds(start, 256)], sems.at[len(copies)]
                )
            )
    return copies


def place_kernel(sides, turns, where, *refs):
    copies = place_copies(sides, turns, where, refs[: len(sides)], refs[-2], refs[-1])
    for copy in copies:
        copy.start()
    for copy in copies:
        copy.wait()


def last_kernel(sides, turns, where, *refs):
    keep, came, _, out, shard, sems = refs[len(sides) :]
    copies = place_copies(sides, turns, where, refs[: len(sides)], out, sems)
    for copy in copies:
        copy.start()
    shard[0] = (keep[...] + came[...].astype(jnp.float32)).astype(jnp.bfloat16)
    for copy in copies:
        copy.wait()


def place_last(where, out, items, keep, came):
    blocks, sides, turns = zip(*items)
    return call(
        functools.partial(last_kernel, sides, turns),
        [bf16(128, 8192), bf16(1, 16, 8192)],
        (where, *blocks, keep, came, out),
        [SMEM] + [VMEM] * (len(blocks) + 2) + [HBM],
        [HBM, VMEM],
        scratch=[pltpu.SemaphoreType.DMA((4 * len(blocks),))],
        cost=1 << 18,
        alias={3 + len(blocks): 0},
    )


def place(where, out, items):
    blocks, sides, turns = zip(*items)
    given = [] if out is None else [out]
    return call(
        functools.partial(place_kernel, sides, turns),
        [bf16(128, 8192)],
        (where, *blocks, *given),
        [SMEM] + [VMEM] * len(blocks) + [HBM] * len(given),
        [HBM],
        scratch=[pltpu.SemaphoreType.DMA((4 * len(blocks),))],
        cost=1 << 18,
        alias={1 + len(blocks): 0} if given else None,
    )[0]


def both_steps(where, pseudo_grad, anchor, momentum, hidden, grad_out):
    mine, give, peak, other_peak = call(
        split_kernel,
        [bf16(16, 128, 256)] * 2 + [bf16(32, 128)] * 2,
        (where, pltpu.with_memory_space_constraint(pseudo_grad, pltpu.HBM)),
        [SMEM, HBM],
        scratch=[
            pltpu.VMEM((128, 8192), jnp.bfloat16),
            pltpu.VMEM((128, 128), jnp.float32),
            pltpu.SemaphoreType.DMA((4,)),
        ],
        cost=1 << 21,
    )
    peak = jnp.maximum(peak, to_core(other_peak))
    (give,) = gate((peak,), give)
    other = to_core(give)
    near = [to_x(peak, k) for k in (1, 2, 3)]
    pieces = inner_pieces(where, hidden, grad_out, peak, 0)
    (peak,) = call(
        top_kernel,
        [bf16(32, 128)],
        (peak, *near, other, pieces[0]),
        [VMEM] * 4 + [ANY] * 2,
        cost=1 << 16,
    )
    peaks = [peak] + [to_z(peak, k) for k in (1, 2, 3)]
    pieces = list(inner_pieces(where, hidden, grad_out, peak, 1, pieces))
    *codes, step = call(
        encode_kernel,
        [bf16(4, 128, 256)] * 4 + [f32(128, 256)],
        (where, mine, other, *peaks, pieces[0]),
        [SMEM] + [VMEM] * 6 + [ANY],
        scratch=[pltpu.VMEM((16, 128, 256), jnp.float32)],
        cost=1 << 22,
    )
    parts = [codes[0]] + [to_x(codes[k], k) for k in (1, 2, 3)]
    pieces[1], pieces[3] = gate((codes[0],), pieces[1], pieces[3])
    pieces[1], pieces[3] = to_y(pieces[1], 1), to_y(pieces[3], 3)
    sums = call(
        sum_x_kernel,
        [f32(128, 256)] + [bf16(128, 256)] * 3,
        (where, *parts),
        [SMEM] + [VMEM] * 4,
        cost=1 << 31,
    )
    (pieces[2],) = gate((sums[0],), pieces[2])
    inner_keep, inner_give = call(
        sum_y_kernel,
        [f32(16, 8192), bf16(16, 8192)],
        (where, pieces[0], pieces[1], to_y(pieces[2], 2), pieces[3]),
        [SMEM] + [VMEM] * 4,
        cost=1 << 21,
    )
    parts = [sums[0]] + [to_z(sums[k], k) for k in (1, 2, 3)]
    anchor_next, momentum_next, params = call(
        update_kernel,
        [f32(128, 256), f32(128, 256), bf16(128, 256)],
        (*parts, step, anchor, momentum, pieces[1], pieces[3]),
        [VMEM] * 7 + [ANY] * 2,
        cost=1 << 32,
    )
    parts = [params] + [to_z(params, k) for k in (1, 2, 3)]
    (block,) = call(
        gather_z_kernel,
        [bf16(4, 128, 256)],
        (where, *parts, inner_give),
        [SMEM] + [VMEM] * 4 + [ANY],
    )
    far = [to_x(block, k) for k in (1, 2, 3)]
    twin = to_core(gate((far[0],), block)[0])
    twins = [to_core(a) for a in far]
    params_next = place(where, None, [(block, 0, 0)] + [(a, 0, k) for k, a in zip((1, 2, 3), far)])
    params_next, grad_shard = place_last(
        where,
        params_next,
        [(a, 1, k) for k, a in zip((0, 1, 2, 3), (twin, *twins))],
        inner_keep,
        to_half(inner_give),
    )
    return anchor_next, momentum_next, params_next, grad_shard


def product_kernel(where, hidden, grad, after, *refs):
    o0, o1, o2, o3, left, whole = refs[-6:]

    @pl.when(pl.program_id(0) == 0)
    def _():
        left[...] = hidden[0].astype(jnp.float32).T.astype(jnp.bfloat16)

    whole[...] = jnp.dot(
        left[...], grad[0], preferred_element_type=jnp.float32
    ).astype(jnp.bfloat16)
    y = where[3]
    for k, out in enumerate((o0, o1, o2, o3)):
        for half in range(2):
            start = pl.multiple_of(half * 64 + lax.rem(y + k, 4) * 16, 16)
            out[half * 16 : half * 16 + 16, :] = whole[pl.ds(start, 16), :]


def sum_y_kernel(where, a0, a1, a2, a3, keep, give):
    half = where[4]
    for side, out in ((half, keep), (1 - half, give)):
        rows = pl.ds(pl.multiple_of(side * 16, 16), 16)
        parts = [a[rows, :].astype(jnp.float32) for a in (a0, a1, a2, a3)]
        out[...] = ((parts[0] + parts[1]) + (parts[2] + parts[3])).astype(out.dtype)


def inner_pieces(where, hidden, grad_out, after, part, given=()):
    tile = 2048
    steps = 8192 // tile // 2
    return pl.pallas_call(
        product_kernel,
        grid=(steps,),
        out_shape=[bf16(32, 8192)] * 4,
        in_specs=[
            SMEM,
            pl.BlockSpec((1, 384, 128), lambda i: (0, 0, 0)),
            pl.BlockSpec((1, 384, tile), lambda i: (0, 0, i + part * steps)),
            ANY,
        ]
        + [ANY] * len(given),
        out_specs=[pl.BlockSpec((32, tile), lambda i: (0, i + part * steps))] * 4,
        scratch_shapes=[
            pltpu.VMEM((128, 384), jnp.bfloat16),
            pltpu.VMEM((128, tile), jnp.bfloat16),
        ],
        input_output_aliases={4 + k: k for k in range(len(given))},
        cost_estimate=pl.CostEstimate(
            flops=128 * 384 * 8192, bytes_accessed=1 << 22, transcendentals=0
        ),
        compiler_params=pltpu.CompilerParams(vmem_limit_bytes=LIMIT),
    )(where, hidden, pltpu.with_memory_space_constraint(grad_out, pltpu.HBM), after, *given)


def on_device(pseudo_grad, anchor, momentum, hidden, grad_out):
    r, f = lax.axis_index("replica"), lax.axis_index("fsdp")
    where = jnp.stack([r & 1, (r >> 1) & 3, r >> 3, f & 3, f >> 2]).astype(jnp.int32)
    return both_steps(where, pseudo_grad, anchor, momentum, hidden, grad_out)


def solution(mesh):
    placed = (
        P("replica", "fsdp", None),
        P("fsdp", "replica"),
        P("fsdp", "replica"),
        P("replica", "fsdp", None),
        P("replica", "fsdp", None),
    )
    return jax.shard_map(
        on_device,
        mesh=mesh,
        in_specs=placed,
        out_specs=(
            P("fsdp", "replica"),
            P("fsdp", "replica"),
            P("fsdp", None),
            P("replica", "fsdp", None),
        ),
        check_vma=False,
    )
```

```python
import functools

import jax
import jax.numpy as jnp
from jax import lax
from jax.experimental import pallas as pl
from jax.experimental.pallas import tpu as pltpu
from jax.sharding import PartitionSpec as P

BLOCK = 128
EPSILON = 1e-06
TOP_EXPONENT = 6
OUTER_MOMENTUM = 0.9
OUTER_RATE = 0.7
LIMIT = 16 * 1024 * 1024

ANY = pl.BlockSpec(memory_space=pl.ANY)
VMEM = pl.BlockSpec(memory_space=pltpu.VMEM)
HBM = pl.BlockSpec(memory_space=pltpu.HBM)
SMEM = pl.BlockSpec(memory_space=pltpu.SMEM)


def replica_perm(move):
    pairs = []
    for z in range(4):
        for x in range(4):
            for c in range(2):
                to = move(z, x, c)
                pairs.append((z * 8 + x * 2 + c, to[0] * 8 + to[1] * 2 + to[2]))
    return pairs


def fsdp_perm(move):
    pairs = []
    for h in range(2):
        for y in range(4):
            to = move(h, y)
            pairs.append((h * 4 + y, to[0] * 4 + to[1]))
    return pairs


def to_core(a):
    return lax.ppermute(a, "replica", replica_perm(lambda z, x, c: (z, x, 1 - c)))


def to_x(a, k):
    return lax.ppermute(a, "replica", replica_perm(lambda z, x, c: (z, (x + k) % 4, c)))


def to_z(a, k):
    return lax.ppermute(a, "replica", replica_perm(lambda z, x, c: (z ^ k, x, c)))


def to_y(a, k):
    return lax.ppermute(a, "fsdp", fsdp_perm(lambda h, y: (h, (y + k) % 4)))


def to_half(a):
    return lax.ppermute(a, "fsdp", fsdp_perm(lambda h, y: (1 - h, y)))


def call(kernel, out, ins, specs, out_specs=None, scratch=(), cost=0, alias=None):
    return pl.pallas_call(
        kernel,
        out_shape=out,
        in_specs=specs,
        out_specs=out_specs if out_specs is not None else [VMEM] * len(out),
        scratch_shapes=list(scratch),
        input_output_aliases=alias or {},
        cost_estimate=pl.CostEstimate(flops=cost, bytes_accessed=cost, transcendentals=0),
        compiler_params=pltpu.CompilerParams(vmem_limit_bytes=LIMIT),
    )(*ins)


def gate_kernel(*refs):
    pass


def gate(after, *arrays):
    n = len(arrays)
    return call(
        gate_kernel,
        [jax.ShapeDtypeStruct(a.shape, a.dtype) for a in arrays],
        (*arrays, *after),
        [ANY] * (n + len(after)),
        [ANY] * n,
        cost=1 << 10,
        alias={i: i for i in range(n)},
    )


def bf16(*shape):
    return jax.ShapeDtypeStruct(shape, jnp.bfloat16)


def f32(*shape):
    return jax.ShapeDtypeStruct(shape, jnp.float32)


def split_kernel(where, grad, keep, give, keep_peak, give_peak, rows, tops, sems):
    core = where[0]

    def fetch(i):
        part = pl.ds(pl.multiple_of(i * 32, 32), 32)
        return pltpu.make_async_copy(grad.at[0, part, :], rows.at[part, :], sems.at[i])

    for i in range(4):
        fetch(i).start()
    lanes = lax.broadcasted_iota(jnp.int32, (32, 128), 1)

    def chunk(i, carry):
        fetch(i).wait()
        part = pl.ds(pl.multiple_of(i * 32, 32), 32)
        acc = jnp.zeros((32, 128), jnp.float32)
        for n in range(16):
            for k, (side, out) in enumerate(((core, keep), (1 - core, give))):
                start = pl.multiple_of(n * 512 + side * 256, 256)
                value = rows[part, pl.ds(start, 256)]
                out[n, part, :] = value
                size = jnp.abs(value)
                for b in range(2):
                    block = size[:, b * BLOCK : (b + 1) * BLOCK].astype(jnp.float32)
                    top = jnp.max(block, axis=1, keepdims=True)
                    acc = jnp.where(lanes == 32 * k + 2 * n + b, top, acc)
        tops[part, :] = acc
        return carry

    lax.fori_loop(0, 4, chunk, 0)
    flat = tops[...].T
    keep_peak[...] = flat[:32].astype(jnp.bfloat16)
    give_peak[...] = flat[32:64].astype(jnp.bfloat16)


def top_kernel(a0, a1, a2, a3, *rest):
    out = rest[-1]
    out[...] = jnp.maximum(jnp.maximum(a0[...], a1[...]), jnp.maximum(a2[...], a3[...]))


def scale_of(peak):
    bounded = peak + EPSILON
    scale = jnp.ones_like(bounded)
    for e in range(1, 26):
        scale = jnp.where(bounded <= 2.0 ** (TOP_EXPONENT - e), 2.0**e, scale)
    return scale


def encode_kernel(where, mine, other, p0, p1, p2, p3, after, o0, o1, o2, o3, step, scales):
    x, z = where[1], where[2]
    peak = jnp.maximum(
        jnp.maximum(p0[...].astype(jnp.float32), p1[...].astype(jnp.float32)),
        jnp.maximum(p2[...].astype(jnp.float32), p3[...].astype(jnp.float32)),
    )
    scale = scale_of(peak)
    wide = jnp.concatenate([scale, jnp.ones((96, 128), jnp.float32)], axis=0).T
    for n in range(32):
        scales[n // 2, :, (n % 2) * BLOCK : (n % 2 + 1) * BLOCK] = jnp.broadcast_to(
            wide[:, n : n + 1], (128, 128)
        )
    step[...] = 1.0 / (scales[z * 4 + x] * 32.0)
    for k, out in enumerate((o0, o1, o2, o3)):
        column = lax.rem(x + k, 4)
        for level in range(4):
            n = level * 4 + column
            s = scales[n]
            first = jnp.floor(mine[n].astype(jnp.float32) * s + 0.5)
            second = jnp.floor(other[n].astype(jnp.float32) * s + 0.5)
            out[level] = (first + second).astype(jnp.bfloat16)


def sum_x_kernel(where, a0, a1, a2, a3, o0, o1, o2, o3):
    z = where[2]
    for k, out in enumerate((o0, o1, o2, o3)):
        level = z ^ k
        parts = [a[level].astype(jnp.float32) for a in (a0, a1, a2, a3)]
        out[...] = (((parts[0] + parts[1]) + (parts[2] + parts[3]))).astype(out.dtype)


def update_kernel(a0, a1, a2, a3, step, anchor, momentum, after1, after2, anchor_out, momentum_out, params):
    parts = [a[...].astype(jnp.float32) for a in (a0, a1, a2, a3)]
    total = (parts[0] + parts[1]) + (parts[2] + parts[3])
    delta = total * step[...]
    fresh = OUTER_MOMENTUM * momentum[...] + delta
    moved = anchor[...] - OUTER_RATE * (delta + OUTER_MOMENTUM * fresh)
    momentum_out[...] = fresh
    anchor_out[...] = moved
    params[...] = moved.astype(jnp.bfloat16)


def gather_z_kernel(where, a0, a1, a2, a3, after, out):
    z = where[2]
    for k, a in enumerate((a0, a1, a2, a3)):
        out[z ^ k] = a[...]


def place_copies(sides, turns, where, blocks, out, sems):
    core, x = where[0], where[1]
    copies = []
    for block, side, turn in zip(blocks, sides, turns):
        column = lax.rem(x + 4 - turn, 4)
        half = core if side == 0 else 1 - core
        for level in range(4):
            start = pl.multiple_of((level * 4 + column) * 512 + half * 256, 256)
            copies.append(
                pltpu.make_async_copy(
                    block.at[level], out.at[:, pl.ds(start, 256)], sems.at[len(copies)]
                )
            )
    return copies


def place_kernel(sides, turns, where, *refs):
    copies = place_copies(sides, turns, where, refs[: len(sides)], refs[-2], refs[-1])
    for copy in copies:
        copy.start()
    for copy in copies:
        copy.wait()


def add_halves_kernel(keep, came, out):
    out[0] = (keep[...] + came[...].astype(jnp.float32)).astype(jnp.bfloat16)


def place(where, out, items):
    blocks, sides, turns = zip(*items)
    given = [] if out is None else [out]
    return call(
        functools.partial(place_kernel, sides, turns),
        [bf16(128, 8192)],
        (where, *blocks, *given),
        [SMEM] + [VMEM] * len(blocks) + [HBM] * len(given),
        [HBM],
        scratch=[pltpu.SemaphoreType.DMA((4 * len(blocks),))],
        cost=1 << 18,
        alias={1 + len(blocks): 0} if given else None,
    )[0]


def both_steps(where, pseudo_grad, anchor, momentum, hidden, grad_out):
    mine, give, peak, other_peak = call(
        split_kernel,
        [bf16(16, 128, 256)] * 2 + [bf16(32, 128)] * 2,
        (where, pltpu.with_memory_space_constraint(pseudo_grad, pltpu.HBM)),
        [SMEM, HBM],
        scratch=[
            pltpu.VMEM((128, 8192), jnp.bfloat16),
            pltpu.VMEM((128, 128), jnp.float32),
            pltpu.SemaphoreType.DMA((4,)),
        ],
        cost=1 << 21,
    )
    peak = jnp.maximum(peak, to_core(other_peak))
    (give,) = gate((peak,), give)
    other = to_core(give)
    near = [to_x(peak, k) for k in (1, 2, 3)]
    pieces = inner_pieces(where, hidden, grad_out, peak, 0)
    (peak,) = call(
        top_kernel,
        [bf16(32, 128)],
        (peak, *near, other, pieces[0]),
        [VMEM] * 4 + [ANY] * 2,
        cost=1 << 16,
    )
    peaks = [peak] + [to_z(peak, k) for k in (1, 2, 3)]
    pieces = list(inner_pieces(where, hidden, grad_out, peak, 1, pieces))
    *codes, step = call(
        encode_kernel,
        [bf16(4, 128, 256)] * 4 + [f32(128, 256)],
        (where, mine, other, *peaks, pieces[0]),
        [SMEM] + [VMEM] * 6 + [ANY],
        scratch=[pltpu.VMEM((16, 128, 256), jnp.float32)],
        cost=1 << 22,
    )
    parts = [codes[0]] + [to_x(codes[k], k) for k in (1, 2, 3)]
    pieces[1], pieces[3] = gate((codes[0],), pieces[1], pieces[3])
    pieces[1], pieces[3] = to_y(pieces[1], 1), to_y(pieces[3], 3)
    sums = call(
        sum_x_kernel,
        [f32(128, 256)] + [bf16(128, 256)] * 3,
        (where, *parts),
        [SMEM] + [VMEM] * 4,
        cost=1 << 31,
    )
    (pieces[2],) = gate((sums[0],), pieces[2])
    inner_keep, inner_give = call(
        sum_y_kernel,
        [f32(16, 8192), bf16(16, 8192)],
        (where, pieces[0], pieces[1], to_y(pieces[2], 2), pieces[3]),
        [SMEM] + [VMEM] * 4,
        cost=1 << 21,
    )
    parts = [sums[0]] + [to_z(sums[k], k) for k in (1, 2, 3)]
    anchor_next, momentum_next, params = call(
        update_kernel,
        [f32(128, 256), f32(128, 256), bf16(128, 256)],
        (*parts, step, anchor, momentum, pieces[1], pieces[3]),
        [VMEM] * 7 + [ANY] * 2,
        cost=1 << 32,
    )
    parts = [params] + [to_z(params, k) for k in (1, 2, 3)]
    (block,) = call(
        gather_z_kernel,
        [bf16(4, 128, 256)],
        (where, *parts, inner_give),
        [SMEM] + [VMEM] * 4 + [ANY],
    )
    far = [to_x(block, k) for k in (1, 2, 3)]
    twin = to_core(block)
    (grad_shard,) = call(
        add_halves_kernel,
        [bf16(1, 16, 8192)],
        (inner_keep, to_half(inner_give)),
        [VMEM] * 2,
        cost=1 << 20,
    )
    twins = [to_core(a) for a in far]
    params_next = place(where, None, [(a, 0, k) for k, a in enumerate([block, *far])])
    params_next = place(where, params_next, [(a, 1, k) for k, a in zip((1, 2, 3, 0), (*twins, twin))])
    return anchor_next, momentum_next, params_next, grad_shard


def product_kernel(where, hidden, grad, after, *refs):
    o0, o1, o2, o3, left, whole = refs[-6:]

    @pl.when(pl.program_id(0) == 0)
    def _():
        left[...] = hidden[0].astype(jnp.float32).T.astype(jnp.bfloat16)

    whole[...] = jnp.dot(
        left[...], grad[0], preferred_element_type=jnp.float32
    ).astype(jnp.bfloat16)
    y = where[3]
    for k, out in enumerate((o0, o1, o2, o3)):
        for half in range(2):
            start = pl.multiple_of(half * 64 + lax.rem(y + k, 4) * 16, 16)
            out[half * 16 : half * 16 + 16, :] = whole[pl.ds(start, 16), :]


def sum_y_kernel(where, a0, a1, a2, a3, keep, give):
    half = where[4]
    for side, out in ((half, keep), (1 - half, give)):
        rows = pl.ds(pl.multiple_of(side * 16, 16), 16)
        parts = [a[rows, :].astype(jnp.float32) for a in (a0, a1, a2, a3)]
        out[...] = ((parts[0] + parts[1]) + (parts[2] + parts[3])).astype(out.dtype)


def inner_pieces(where, hidden, grad_out, after, part, given=()):
    tile = 2048
    steps = 8192 // tile // 2
    return pl.pallas_call(
        product_kernel,
        grid=(steps,),
        out_shape=[bf16(32, 8192)] * 4,
        in_specs=[
            SMEM,
            pl.BlockSpec((1, 384, 128), lambda i: (0, 0, 0)),
            pl.BlockSpec((1, 384, tile), lambda i: (0, 0, i + part * steps)),
            ANY,
        ]
        + [ANY] * len(given),
        out_specs=[pl.BlockSpec((32, tile), lambda i: (0, i + part * steps))] * 4,
        scratch_shapes=[
            pltpu.VMEM((128, 384), jnp.bfloat16),
            pltpu.VMEM((128, tile), jnp.bfloat16),
        ],
        input_output_aliases={4 + k: k for k in range(len(given))},
        cost_estimate=pl.CostEstimate(
            flops=128 * 384 * 8192, bytes_accessed=1 << 22, transcendentals=0
        ),
        compiler_params=pltpu.CompilerParams(vmem_limit_bytes=LIMIT),
    )(where, hidden, pltpu.with_memory_space_constraint(grad_out, pltpu.HBM), after, *given)


def on_device(pseudo_grad, anchor, momentum, hidden, grad_out):
    r, f = lax.axis_index("replica"), lax.axis_index("fsdp")
    where = jnp.stack([r & 1, (r >> 1) & 3, r >> 3, f & 3, f >> 2]).astype(jnp.int32)
    return both_steps(where, pseudo_grad, anchor, momentum, hidden, grad_out)


def solution(mesh):
    placed = (
        P("replica", "fsdp", None),
        P("fsdp", "replica"),
        P("fsdp", "replica"),
        P("replica", "fsdp", None),
        P("replica", "fsdp", None),
    )
    return jax.shard_map(
        on_device,
        mesh=mesh,
        in_specs=placed,
        out_specs=(
            P("fsdp", "replica"),
            P("fsdp", "replica"),
            P("fsdp", None),
            P("replica", "fsdp", None),
        ),
        check_vma=False,
    )
```

```python
import functools

import jax
import jax.numpy as jnp
from jax import lax
from jax.experimental import pallas as pl
from jax.experimental.pallas import tpu as pltpu
from jax.sharding import PartitionSpec as P

BLOCK = 128
EPSILON = 1e-06
TOP_EXPONENT = 6
OUTER_MOMENTUM = 0.9
OUTER_RATE = 0.7
LIMIT = 16 * 1024 * 1024

ANY = pl.BlockSpec(memory_space=pl.ANY)
VMEM = pl.BlockSpec(memory_space=pltpu.VMEM)
HBM = pl.BlockSpec(memory_space=pltpu.HBM)
SMEM = pl.BlockSpec(memory_space=pltpu.SMEM)


def replica_perm(move):
    pairs = []
    for z in range(4):
        for x in range(4):
            for c in range(2):
                to = move(z, x, c)
                pairs.append((z * 8 + x * 2 + c, to[0] * 8 + to[1] * 2 + to[2]))
    return pairs


def fsdp_perm(move):
    pairs = []
    for h in range(2):
        for y in range(4):
            to = move(h, y)
            pairs.append((h * 4 + y, to[0] * 4 + to[1]))
    return pairs


def to_core(a):
    return lax.ppermute(a, "replica", replica_perm(lambda z, x, c: (z, x, 1 - c)))


def to_x(a, k):
    return lax.ppermute(a, "replica", replica_perm(lambda z, x, c: (z, (x + k) % 4, c)))


def to_z(a, k):
    return lax.ppermute(a, "replica", replica_perm(lambda z, x, c: (z ^ k, x, c)))


def to_y(a, k):
    return lax.ppermute(a, "fsdp", fsdp_perm(lambda h, y: (h, (y + k) % 4)))


def to_half(a):
    return lax.ppermute(a, "fsdp", fsdp_perm(lambda h, y: (1 - h, y)))


def call(kernel, out, ins, specs, out_specs=None, scratch=(), cost=0, alias=None):
    return pl.pallas_call(
        kernel,
        out_shape=out,
        in_specs=specs,
        out_specs=out_specs if out_specs is not None else [VMEM] * len(out),
        scratch_shapes=list(scratch),
        input_output_aliases=alias or {},
        cost_estimate=pl.CostEstimate(flops=cost, bytes_accessed=cost, transcendentals=0),
        compiler_params=pltpu.CompilerParams(vmem_limit_bytes=LIMIT),
    )(*ins)


def gate_kernel(*refs):
    pass


def gate(after, *arrays, cost=1 << 10):
    n = len(arrays)
    return call(
        gate_kernel,
        [jax.ShapeDtypeStruct(a.shape, a.dtype) for a in arrays],
        (*arrays, *after),
        [ANY] * (n + len(after)),
        [ANY] * n,
        cost=cost,
        alias={i: i for i in range(n)},
    )


def bf16(*shape):
    return jax.ShapeDtypeStruct(shape, jnp.bfloat16)


def f32(*shape):
    return jax.ShapeDtypeStruct(shape, jnp.float32)


def split_kernel(where, grad, keep, give, keep_peak, give_peak, rows, tops, sems):
    core = where[0]

    def fetch(i):
        part = pl.ds(pl.multiple_of(i * 32, 32), 32)
        return pltpu.make_async_copy(grad.at[0, part, :], rows.at[part, :], sems.at[i])

    for i in range(4):
        fetch(i).start()
    lanes = lax.broadcasted_iota(jnp.int32, (32, 128), 1)

    def chunk(i, carry):
        fetch(i).wait()
        part = pl.ds(pl.multiple_of(i * 32, 32), 32)
        acc = jnp.zeros((32, 128), jnp.float32)
        for n in range(16):
            for k, (side, out) in enumerate(((core, keep), (1 - core, give))):
                start = pl.multiple_of(n * 512 + side * 256, 256)
                value = rows[part, pl.ds(start, 256)]
                out[n, part, :] = value
                size = jnp.abs(value)
                for b in range(2):
                    block = size[:, b * BLOCK : (b + 1) * BLOCK].astype(jnp.float32)
                    top = jnp.max(block, axis=1, keepdims=True)
                    acc = jnp.where(lanes == 32 * k + 2 * n + b, top, acc)
        tops[part, :] = acc
        return carry

    lax.fori_loop(0, 4, chunk, 0)
    flat = tops[...].T
    keep_peak[...] = flat[:32].astype(jnp.bfloat16)
    give_peak[...] = flat[32:64].astype(jnp.bfloat16)


def top_kernel(a0, a1, a2, a3, *rest):
    out = rest[-1]
    out[...] = jnp.maximum(jnp.maximum(a0[...], a1[...]), jnp.maximum(a2[...], a3[...]))


def scale_of(peak):
    bounded = peak + EPSILON
    scale = jnp.ones_like(bounded)
    for e in range(1, 26):
        scale = jnp.where(bounded <= 2.0 ** (TOP_EXPONENT - e), 2.0**e, scale)
    return scale


def encode_kernel(where, mine, other, p0, p1, p2, p3, after, o0, o1, o2, o3, step, scales):
    x, z = where[1], where[2]
    peak = jnp.maximum(
        jnp.maximum(p0[...].astype(jnp.float32), p1[...].astype(jnp.float32)),
        jnp.maximum(p2[...].astype(jnp.float32), p3[...].astype(jnp.float32)),
    )
    scale = scale_of(peak)
    wide = jnp.concatenate([scale, jnp.ones((96, 128), jnp.float32)], axis=0).T
    for n in range(32):
        scales[n // 2, :, (n % 2) * BLOCK : (n % 2 + 1) * BLOCK] = jnp.broadcast_to(
            wide[:, n : n + 1], (128, 128)
        )
    step[...] = 1.0 / (scales[z * 4 + x] * 32.0)
    for k, out in enumerate((o0, o1, o2, o3)):
        column = lax.rem(x + k, 4)
        for level in range(4):
            n = level * 4 + column
            s = scales[n]
            first = jnp.floor(mine[n].astype(jnp.float32) * s + 0.5)
            second = jnp.floor(other[n].astype(jnp.float32) * s + 0.5)
            out[level] = (first + second).astype(jnp.bfloat16)


def sum_x_kernel(where, a0, a1, a2, a3, o0, o1, o2, o3):
    z = where[2]
    for k, out in enumerate((o0, o1, o2, o3)):
        level = z ^ k
        parts = [a[level].astype(jnp.float32) for a in (a0, a1, a2, a3)]
        out[...] = (((parts[0] + parts[1]) + (parts[2] + parts[3]))).astype(out.dtype)


def update_kernel(a0, a1, a2, a3, step, anchor, momentum, after1, after2, anchor_out, momentum_out, params):
    parts = [a[...].astype(jnp.float32) for a in (a0, a1, a2, a3)]
    total = (parts[0] + parts[1]) + (parts[2] + parts[3])
    delta = total * step[...]
    fresh = OUTER_MOMENTUM * momentum[...] + delta
    moved = anchor[...] - OUTER_RATE * (delta + OUTER_MOMENTUM * fresh)
    momentum_out[...] = fresh
    anchor_out[...] = moved
    params[...] = moved.astype(jnp.bfloat16)


def gather_z_kernel(where, a0, a1, a2, a3, after, out):
    z = where[2]
    for k, a in enumerate((a0, a1, a2, a3)):
        out[z ^ k] = a[...]


def place_copies(sides, turns, where, blocks, out, sems):
    core, x = where[0], where[1]
    copies = []
    for block, side, turn in zip(blocks, sides, turns):
        column = lax.rem(x + 4 - turn, 4)
        half = core if side == 0 else 1 - core
        for level in range(4):
            start = pl.multiple_of((level * 4 + column) * 512 + half * 256, 256)
            copies.append(
                pltpu.make_async_copy(
                    block.at[level], out.at[:, pl.ds(start, 256)], sems.at[len(copies)]
                )
            )
    return copies


def place_kernel(sides, turns, where, *refs):
    out, token, sems = refs[-3:]
    copies = place_copies(sides, turns, where, refs[: len(sides)], out, sems)
    for copy in copies:
        copy.start()
    for copy in copies:
        copy.wait()
    token[...] = jnp.zeros_like(token)


def last_kernel(sides, turns, where, keep, came, *refs):
    blocks, (_, out, shard, total, sem, sems) = refs[: len(sides)], refs[len(sides) :]
    copies = place_copies(sides, turns, where, blocks, out, sems)
    for copy in copies:
        copy.start()
    total[...] = (keep[...] + came[...].astype(jnp.float32)).astype(jnp.bfloat16)
    copies.append(pltpu.make_async_copy(total, shard.at[0], sem))
    copies[-1].start()
    for copy in copies:
        copy.wait()


def place_last(where, out, items, keep, came):
    blocks, sides, turns = zip(*items)
    return call(
        functools.partial(last_kernel, sides, turns),
        [bf16(128, 8192), bf16(1, 16, 8192)],
        (where, keep, came, *blocks, out),
        [SMEM] + [VMEM] * (len(blocks) + 2) + [HBM],
        [HBM, HBM],
        scratch=[
            pltpu.VMEM((16, 8192), jnp.bfloat16),
            pltpu.SemaphoreType.DMA,
            pltpu.SemaphoreType.DMA((4 * len(blocks),)),
        ],
        cost=1 << 18,
        alias={3 + len(blocks): 0},
    )


def place(where, out, items):
    blocks, sides, turns = zip(*items)
    given = [] if out is None else [out]
    return call(
        functools.partial(place_kernel, sides, turns),
        [bf16(128, 8192), f32(8, 128)],
        (where, *blocks, *given),
        [SMEM] + [VMEM] * len(blocks) + [HBM] * len(given),
        [HBM, VMEM],
        scratch=[pltpu.SemaphoreType.DMA((4 * len(blocks),))],
        cost=1 << 18,
        alias={1 + len(blocks): 0} if given else None,
    )


def both_steps(where, pseudo_grad, anchor, momentum, hidden, grad_out):
    mine, give, peak, other_peak = call(
        split_kernel,
        [bf16(16, 128, 256)] * 2 + [bf16(32, 128)] * 2,
        (where, pltpu.with_memory_space_constraint(pseudo_grad, pltpu.HBM)),
        [SMEM, HBM],
        scratch=[
            pltpu.VMEM((128, 8192), jnp.bfloat16),
            pltpu.VMEM((128, 128), jnp.float32),
            pltpu.SemaphoreType.DMA((4,)),
        ],
        cost=1 << 21,
    )
    peak = jnp.maximum(peak, to_core(other_peak))
    (give,) = gate((peak,), give)
    other = to_core(give)
    near = [to_x(peak, k) for k in (1, 2, 3)]
    pieces = inner_pieces(where, hidden, grad_out, peak, 0)
    (peak,) = call(
        top_kernel,
        [bf16(32, 128)],
        (peak, *near, other, pieces[0]),
        [VMEM] * 4 + [ANY] * 2,
        cost=1 << 16,
    )
    peaks = [peak] + [to_z(peak, k) for k in (1, 2, 3)]
    pieces = list(inner_pieces(where, hidden, grad_out, peak, 1, pieces))
    *codes, step = call(
        encode_kernel,
        [bf16(4, 128, 256)] * 4 + [f32(128, 256)],
        (where, mine, other, *peaks, pieces[0]),
        [SMEM] + [VMEM] * 6 + [ANY],
        scratch=[pltpu.VMEM((16, 128, 256), jnp.float32)],
        cost=1 << 22,
    )
    parts = [codes[0]] + [to_x(codes[k], k) for k in (1, 2, 3)]
    pieces[1], pieces[3] = gate((codes[0],), pieces[1], pieces[3])
    pieces[1], pieces[3] = to_y(pieces[1], 1), to_y(pieces[3], 3)
    sums = call(
        sum_x_kernel,
        [f32(128, 256)] + [bf16(128, 256)] * 3,
        (where, *parts),
        [SMEM] + [VMEM] * 4,
        cost=1 << 31,
    )
    (pieces[2],) = gate((sums[0],), pieces[2])
    inner_keep, inner_give = call(
        sum_y_kernel,
        [f32(16, 8192), bf16(16, 8192)],
        (where, pieces[0], pieces[1], to_y(pieces[2], 2), pieces[3]),
        [SMEM] + [VMEM] * 4,
        cost=1 << 21,
    )
    parts = [sums[0]] + [to_z(sums[k], k) for k in (1, 2, 3)]
    anchor_next, momentum_next, params = call(
        update_kernel,
        [f32(128, 256), f32(128, 256), bf16(128, 256)],
        (*parts, step, anchor, momentum, pieces[1], pieces[3]),
        [VMEM] * 7 + [ANY] * 2,
        cost=1 << 32,
    )
    parts = [params] + [to_z(params, k) for k in (1, 2, 3)]
    (block,) = call(
        gather_z_kernel,
        [bf16(4, 128, 256)],
        (where, *parts, inner_give),
        [SMEM] + [VMEM] * 4 + [ANY],
    )
    twin = to_core(block)
    far = [to_x(block, k) for k in (1, 2, 3)]
    twins = [to_core(a) for a in far]
    params_next, token = place(where, None, [(a, 0, k) for k, a in enumerate([block, *far])])
    (came,) = gate((token,), to_half(inner_give), cost=1 << 21)
    params_next, grad_shard = place_last(
        where,
        params_next,
        [(a, 1, k) for k, a in zip((1, 2, 3, 0), (*twins, twin))],
        inner_keep,
        came,
    )
    return anchor_next, momentum_next, params_next, grad_shard


def product_kernel(where, hidden, grad, after, *refs):
    o0, o1, o2, o3, left, whole = refs[-6:]

    @pl.when(pl.program_id(0) == 0)
    def _():
        left[...] = hidden[0].astype(jnp.float32).T.astype(jnp.bfloat16)

    whole[...] = jnp.dot(
        left[...], grad[0], preferred_element_type=jnp.float32
    ).astype(jnp.bfloat16)
    y = where[3]
    for k, out in enumerate((o0, o1, o2, o3)):
        for half in range(2):
            start = pl.multiple_of(half * 64 + lax.rem(y + k, 4) * 16, 16)
            out[half * 16 : half * 16 + 16, :] = whole[pl.ds(start, 16), :]


def sum_y_kernel(where, a0, a1, a2, a3, keep, give):
    half = where[4]
    for side, out in ((half, keep), (1 - half, give)):
        rows = pl.ds(pl.multiple_of(side * 16, 16), 16)
        parts = [a[rows, :].astype(jnp.float32) for a in (a0, a1, a2, a3)]
        out[...] = ((parts[0] + parts[1]) + (parts[2] + parts[3])).astype(out.dtype)


def inner_pieces(where, hidden, grad_out, after, part, given=()):
    tile = 2048
    steps = 8192 // tile // 2
    return pl.pallas_call(
        product_kernel,
        grid=(steps,),
        out_shape=[bf16(32, 8192)] * 4,
        in_specs=[
            SMEM,
            pl.BlockSpec((1, 384, 128), lambda i: (0, 0, 0)),
            pl.BlockSpec((1, 384, tile), lambda i: (0, 0, i + part * steps)),
            ANY,
        ]
        + [ANY] * len(given),
        out_specs=[pl.BlockSpec((32, tile), lambda i: (0, i + part * steps))] * 4,
        scratch_shapes=[
            pltpu.VMEM((128, 384), jnp.bfloat16),
            pltpu.VMEM((128, tile), jnp.bfloat16),
        ],
        input_output_aliases={4 + k: k for k in range(len(given))},
        cost_estimate=pl.CostEstimate(
            flops=128 * 384 * 8192, bytes_accessed=1 << 22, transcendentals=0
        ),
        compiler_params=pltpu.CompilerParams(vmem_limit_bytes=LIMIT),
    )(where, hidden, pltpu.with_memory_space_constraint(grad_out, pltpu.HBM), after, *given)


def on_device(pseudo_grad, anchor, momentum, hidden, grad_out):
    r, f = lax.axis_index("replica"), lax.axis_index("fsdp")
    where = jnp.stack([r & 1, (r >> 1) & 3, r >> 3, f & 3, f >> 2]).astype(jnp.int32)
    return both_steps(where, pseudo_grad, anchor, momentum, hidden, grad_out)


def solution(mesh):
    placed = (
        P("replica", "fsdp", None),
        P("fsdp", "replica"),
        P("fsdp", "replica"),
        P("replica", "fsdp", None),
        P("replica", "fsdp", None),
    )
    return jax.shard_map(
        on_device,
        mesh=mesh,
        in_specs=placed,
        out_specs=(
            P("fsdp", "replica"),
            P("fsdp", "replica"),
            P("fsdp", None),
            P("replica", "fsdp", None),
        ),
        check_vma=False,
    )
```

```python
import functools

import jax
import jax.numpy as jnp
from jax import lax
from jax.experimental import pallas as pl
from jax.experimental.pallas import tpu as pltpu
from jax.sharding import PartitionSpec as P

BLOCK = 128
EPSILON = 1e-06
TOP_EXPONENT = 6
OUTER_MOMENTUM = 0.9
OUTER_RATE = 0.7
LIMIT = 16 * 1024 * 1024

ANY = pl.BlockSpec(memory_space=pl.ANY)
VMEM = pl.BlockSpec(memory_space=pltpu.VMEM)
HBM = pl.BlockSpec(memory_space=pltpu.HBM)
SMEM = pl.BlockSpec(memory_space=pltpu.SMEM)


def replica_perm(move):
    pairs = []
    for z in range(4):
        for x in range(4):
            for c in range(2):
                to = move(z, x, c)
                pairs.append((z * 8 + x * 2 + c, to[0] * 8 + to[1] * 2 + to[2]))
    return pairs


def fsdp_perm(move):
    pairs = []
    for h in range(2):
        for y in range(4):
            to = move(h, y)
            pairs.append((h * 4 + y, to[0] * 4 + to[1]))
    return pairs


def to_core(a):
    return lax.ppermute(a, "replica", replica_perm(lambda z, x, c: (z, x, 1 - c)))


def to_x(a, k):
    return lax.ppermute(a, "replica", replica_perm(lambda z, x, c: (z, (x + k) % 4, c)))


def to_z(a, k):
    return lax.ppermute(a, "replica", replica_perm(lambda z, x, c: (z ^ k, x, c)))


def to_y(a, k):
    return lax.ppermute(a, "fsdp", fsdp_perm(lambda h, y: (h, (y + k) % 4)))


def to_half(a):
    return lax.ppermute(a, "fsdp", fsdp_perm(lambda h, y: (1 - h, y)))


def call(kernel, out, ins, specs, out_specs=None, scratch=(), cost=0, alias=None):
    return pl.pallas_call(
        kernel,
        out_shape=out,
        in_specs=specs,
        out_specs=out_specs if out_specs is not None else [VMEM] * len(out),
        scratch_shapes=list(scratch),
        input_output_aliases=alias or {},
        cost_estimate=pl.CostEstimate(flops=cost, bytes_accessed=cost, transcendentals=0),
        compiler_params=pltpu.CompilerParams(vmem_limit_bytes=LIMIT),
    )(*ins)


def gate_kernel(*refs):
    pass


def gate(after, *arrays, cost=1 << 10):
    n = len(arrays)
    return call(
        gate_kernel,
        [jax.ShapeDtypeStruct(a.shape, a.dtype) for a in arrays],
        (*arrays, *after),
        [ANY] * (n + len(after)),
        [ANY] * n,
        cost=cost,
        alias={i: i for i in range(n)},
    )


def bf16(*shape):
    return jax.ShapeDtypeStruct(shape, jnp.bfloat16)


def f32(*shape):
    return jax.ShapeDtypeStruct(shape, jnp.float32)


def split_kernel(where, grad, keep, give, keep_peak, give_peak, rows, tops, sems):
    core = where[0]

    def fetch(i):
        part = pl.ds(pl.multiple_of(i * 32, 32), 32)
        return pltpu.make_async_copy(grad.at[0, part, :], rows.at[part, :], sems.at[i])

    for i in range(4):
        fetch(i).start()
    lanes = lax.broadcasted_iota(jnp.int32, (32, 128), 1)

    def chunk(i, carry):
        fetch(i).wait()
        part = pl.ds(pl.multiple_of(i * 32, 32), 32)
        acc = jnp.zeros((32, 128), jnp.float32)
        for n in range(16):
            for k, (side, out) in enumerate(((core, keep), (1 - core, give))):
                start = pl.multiple_of(n * 512 + side * 256, 256)
                value = rows[part, pl.ds(start, 256)]
                out[n, part, :] = value
                size = jnp.abs(value)
                for b in range(2):
                    block = size[:, b * BLOCK : (b + 1) * BLOCK].astype(jnp.float32)
                    top = jnp.max(block, axis=1, keepdims=True)
                    acc = jnp.where(lanes == 32 * k + 2 * n + b, top, acc)
        tops[part, :] = acc
        return carry

    lax.fori_loop(0, 4, chunk, 0)
    flat = tops[...].T
    keep_peak[...] = flat[:32].astype(jnp.bfloat16)
    give_peak[...] = flat[32:64].astype(jnp.bfloat16)


def top_kernel(a0, a1, a2, a3, *rest):
    out = rest[-1]
    out[...] = jnp.maximum(jnp.maximum(a0[...], a1[...]), jnp.maximum(a2[...], a3[...]))


def scale_of(peak):
    bounded = peak + EPSILON
    scale = jnp.ones_like(bounded)
    for e in range(1, 26):
        scale = jnp.where(bounded <= 2.0 ** (TOP_EXPONENT - e), 2.0**e, scale)
    return scale


def encode_kernel(where, mine, other, p0, p1, p2, p3, after, o0, o1, o2, o3, step, scales):
    x, z = where[1], where[2]
    peak = jnp.maximum(
        jnp.maximum(p0[...].astype(jnp.float32), p1[...].astype(jnp.float32)),
        jnp.maximum(p2[...].astype(jnp.float32), p3[...].astype(jnp.float32)),
    )
    scale = scale_of(peak)
    wide = jnp.concatenate([scale, jnp.ones((96, 128), jnp.float32)], axis=0).T
    for n in range(32):
        scales[n // 2, :, (n % 2) * BLOCK : (n % 2 + 1) * BLOCK] = jnp.broadcast_to(
            wide[:, n : n + 1], (128, 128)
        )
    step[...] = 1.0 / (scales[z * 4 + x] * 32.0)
    for k, out in enumerate((o0, o1, o2, o3)):
        column = lax.rem(x + k, 4)
        for level in range(4):
            n = level * 4 + column
            s = scales[n]
            first = jnp.floor(mine[n].astype(jnp.float32) * s + 0.5)
            second = jnp.floor(other[n].astype(jnp.float32) * s + 0.5)
            out[level] = (first + second).astype(jnp.bfloat16)


def sum_x_kernel(where, a0, a1, a2, a3, o0, o1, o2, o3):
    z = where[2]
    for k, out in enumerate((o0, o1, o2, o3)):
        level = z ^ k
        parts = [a[level].astype(jnp.float32) for a in (a0, a1, a2, a3)]
        out[...] = (((parts[0] + parts[1]) + (parts[2] + parts[3]))).astype(out.dtype)


def update_kernel(a0, a1, a2, a3, step, anchor, momentum, after1, after2, anchor_out, momentum_out, params):
    parts = [a[...].astype(jnp.float32) for a in (a0, a1, a2, a3)]
    total = (parts[0] + parts[1]) + (parts[2] + parts[3])
    delta = total * step[...]
    fresh = OUTER_MOMENTUM * momentum[...] + delta
    moved = anchor[...] - OUTER_RATE * (delta + OUTER_MOMENTUM * fresh)
    momentum_out[...] = fresh
    anchor_out[...] = moved
    params[...] = moved.astype(jnp.bfloat16)


def gather_z_kernel(where, a0, a1, a2, a3, after, out):
    z = where[2]
    for k, a in enumerate((a0, a1, a2, a3)):
        out[z ^ k] = a[...]


def place_copies(sides, turns, where, blocks, out, sems):
    core, x = where[0], where[1]
    copies = []
    for block, side, turn in zip(blocks, sides, turns):
        column = lax.rem(x + 4 - turn, 4)
        half = core if side == 0 else 1 - core
        for level in range(4):
            start = pl.multiple_of((level * 4 + column) * 512 + half * 256, 256)
            copies.append(
                pltpu.make_async_copy(
                    block.at[level], out.at[:, pl.ds(start, 256)], sems.at[len(copies)]
                )
            )
    return copies


def place_kernel(sides, turns, where, *refs):
    out, token, sems = refs[-3:]
    copies = place_copies(sides, turns, where, refs[: len(sides)], out, sems)
    for copy in copies:
        copy.start()
    for copy in copies:
        copy.wait()
    token[...] = jnp.zeros_like(token)


def last_kernel(sides, turns, where, keep, came, *refs):
    blocks, (_, out, shard, total, sem, sems) = refs[: len(sides)], refs[len(sides) :]
    copies = place_copies(sides, turns, where, blocks, out, sems)
    for copy in copies:
        copy.start()
    total[...] = (keep[...] + came[...].astype(jnp.float32)).astype(jnp.bfloat16)
    copies.append(pltpu.make_async_copy(total, shard.at[0], sem))
    copies[-1].start()
    for copy in copies:
        copy.wait()


def place_last(where, out, items, keep, came):
    blocks, sides, turns = zip(*items)
    return call(
        functools.partial(last_kernel, sides, turns),
        [bf16(128, 8192), bf16(1, 16, 8192)],
        (where, keep, came, *blocks, out),
        [SMEM] + [VMEM] * (len(blocks) + 2) + [HBM],
        [HBM, HBM],
        scratch=[
            pltpu.VMEM((16, 8192), jnp.bfloat16),
            pltpu.SemaphoreType.DMA,
            pltpu.SemaphoreType.DMA((4 * len(blocks),)),
        ],
        cost=1 << 18,
        alias={3 + len(blocks): 0},
    )


def place(where, out, items):
    blocks, sides, turns = zip(*items)
    given = [] if out is None else [out]
    return call(
        functools.partial(place_kernel, sides, turns),
        [bf16(128, 8192), f32(8, 128)],
        (where, *blocks, *given),
        [SMEM] + [VMEM] * len(blocks) + [HBM] * len(given),
        [HBM, VMEM],
        scratch=[pltpu.SemaphoreType.DMA((4 * len(blocks),))],
        cost=1 << 18,
        alias={1 + len(blocks): 0} if given else None,
    )


def both_steps(where, pseudo_grad, anchor, momentum, hidden, grad_out):
    mine, give, peak, other_peak = call(
        split_kernel,
        [bf16(16, 128, 256)] * 2 + [bf16(32, 128)] * 2,
        (where, pltpu.with_memory_space_constraint(pseudo_grad, pltpu.HBM)),
        [SMEM, HBM],
        scratch=[
            pltpu.VMEM((128, 8192), jnp.bfloat16),
            pltpu.VMEM((128, 128), jnp.float32),
            pltpu.SemaphoreType.DMA((4,)),
        ],
        cost=1 << 21,
    )
    peak = jnp.maximum(peak, to_core(other_peak))
    (give,) = gate((peak,), give)
    other = to_core(give)
    near = [to_x(peak, k) for k in (1, 2, 3)]
    pieces = inner_pieces(where, hidden, grad_out, peak, 0)
    (peak,) = call(
        top_kernel,
        [bf16(32, 128)],
        (peak, *near, other, pieces[0]),
        [VMEM] * 4 + [ANY] * 2,
        cost=1 << 16,
    )
    peaks = [peak] + [to_z(peak, k) for k in (1, 2, 3)]
    pieces = list(inner_pieces(where, hidden, grad_out, peak, 1, pieces))
    *codes, step = call(
        encode_kernel,
        [bf16(4, 128, 256)] * 4 + [f32(128, 256)],
        (where, mine, other, *peaks, pieces[0]),
        [SMEM] + [VMEM] * 6 + [ANY],
        scratch=[pltpu.VMEM((16, 128, 256), jnp.float32)],
        cost=1 << 22,
    )
    parts = [codes[0]] + [to_x(codes[k], k) for k in (2, 1, 3)]
    pieces[1], pieces[3] = gate((codes[0],), pieces[1], pieces[3])
    pieces[1], pieces[3] = to_y(pieces[1], 1), to_y(pieces[3], 3)
    sums = call(
        sum_x_kernel,
        [f32(128, 256)] + [bf16(128, 256)] * 3,
        (where, *parts),
        [SMEM] + [VMEM] * 4,
        cost=1 << 31,
    )
    (pieces[2],) = gate((sums[0],), pieces[2])
    inner_keep, inner_give = call(
        sum_y_kernel,
        [f32(16, 8192), bf16(16, 8192)],
        (where, pieces[0], pieces[1], to_y(pieces[2], 2), pieces[3]),
        [SMEM] + [VMEM] * 4,
        cost=1 << 21,
    )
    parts = [sums[0]] + [to_z(sums[k], k) for k in (1, 2, 3)]
    anchor_next, momentum_next, params = call(
        update_kernel,
        [f32(128, 256), f32(128, 256), bf16(128, 256)],
        (*parts, step, anchor, momentum, pieces[1], pieces[3]),
        [VMEM] * 7 + [ANY] * 2,
        cost=1 << 32,
    )
    parts = [params] + [to_z(params, k) for k in (1, 2, 3)]
    (block,) = call(
        gather_z_kernel,
        [bf16(4, 128, 256)],
        (where, *parts, inner_give),
        [SMEM] + [VMEM] * 4 + [ANY],
    )
    twin = to_core(block)
    far = [to_x(block, k) for k in (1, 2, 3)]
    twins = [to_core(a) for a in far]
    params_next, token = place(where, None, [(a, 0, k) for k, a in enumerate([block, *far])])
    (came,) = gate((token,), to_half(inner_give), cost=1 << 21)
    params_next, grad_shard = place_last(
        where,
        params_next,
        [(a, 1, k) for k, a in zip((1, 2, 3, 0), (*twins, twin))],
        inner_keep,
        came,
    )
    return anchor_next, momentum_next, params_next, grad_shard


def product_kernel(where, hidden, grad, after, *refs):
    o0, o1, o2, o3, left, whole = refs[-6:]

    @pl.when(pl.program_id(0) == 0)
    def _():
        left[...] = hidden[0].astype(jnp.float32).T.astype(jnp.bfloat16)

    whole[...] = jnp.dot(
        left[...], grad[0], preferred_element_type=jnp.float32
    ).astype(jnp.bfloat16)
    y = where[3]
    for k, out in enumerate((o0, o1, o2, o3)):
        for half in range(2):
            start = pl.multiple_of(half * 64 + lax.rem(y + k, 4) * 16, 16)
            out[half * 16 : half * 16 + 16, :] = whole[pl.ds(start, 16), :]


def sum_y_kernel(where, a0, a1, a2, a3, keep, give):
    half = where[4]
    for side, out in ((half, keep), (1 - half, give)):
        rows = pl.ds(pl.multiple_of(side * 16, 16), 16)
        parts = [a[rows, :].astype(jnp.float32) for a in (a0, a1, a2, a3)]
        out[...] = ((parts[0] + parts[1]) + (parts[2] + parts[3])).astype(out.dtype)


def inner_pieces(where, hidden, grad_out, after, part, given=()):
    tile = 2048
    steps = 8192 // tile // 2
    return pl.pallas_call(
        product_kernel,
        grid=(steps,),
        out_shape=[bf16(32, 8192)] * 4,
        in_specs=[
            SMEM,
            pl.BlockSpec((1, 384, 128), lambda i: (0, 0, 0)),
            pl.BlockSpec((1, 384, tile), lambda i: (0, 0, i + part * steps)),
            ANY,
        ]
        + [ANY] * len(given),
        out_specs=[pl.BlockSpec((32, tile), lambda i: (0, i + part * steps))] * 4,
        scratch_shapes=[
            pltpu.VMEM((128, 384), jnp.bfloat16),
            pltpu.VMEM((128, tile), jnp.bfloat16),
        ],
        input_output_aliases={4 + k: k for k in range(len(given))},
        cost_estimate=pl.CostEstimate(
            flops=128 * 384 * 8192, bytes_accessed=1 << 22, transcendentals=0
        ),
        compiler_params=pltpu.CompilerParams(vmem_limit_bytes=LIMIT),
    )(where, hidden, pltpu.with_memory_space_constraint(grad_out, pltpu.HBM), after, *given)


def on_device(pseudo_grad, anchor, momentum, hidden, grad_out):
    r, f = lax.axis_index("replica"), lax.axis_index("fsdp")
    where = jnp.stack([r & 1, (r >> 1) & 3, r >> 3, f & 3, f >> 2]).astype(jnp.int32)
    return both_steps(where, pseudo_grad, anchor, momentum, hidden, grad_out)


def solution(mesh):
    placed = (
        P("replica", "fsdp", None),
        P("fsdp", "replica"),
        P("fsdp", "replica"),
        P("replica", "fsdp", None),
        P("replica", "fsdp", None),
    )
    return jax.shard_map(
        on_device,
        mesh=mesh,
        in_specs=placed,
        out_specs=(
            P("fsdp", "replica"),
            P("fsdp", "replica"),
            P("fsdp", None),
            P("replica", "fsdp", None),
        ),
        check_vma=False,
    )
```
